32 devices in a mesh: copy: 16 (over z, y, core), table: 2 (over x).
Axes of the slice: x: 2, y: 2, z: 4, core: 2. Of those that a mesh axis runs over, the one named last changes fastest.
Arguments:
- pooled: bfloat16 [4096, 28, 128], P('copy', 'table'), may hold values from -6 to 6
- slot_of_table: int32 [26], replicated, may hold values from 0 to 27, as said below
- partner: int32 [16], replicated, may hold values from 0 to 15, as said below
- labels: int32 [4096], P('copy'), may hold values 0 or 1
- w_first: bfloat16 [16, 3328, 4096], P('copy', None, 'table'), may hold values from -0.109375 to 0.109375
- b_first: bfloat16 [16, 4096], P('copy', 'table'), may hold values from -3 to 3
- w_head: bfloat16 [16, 4096], P('copy', 'table'), may hold values from -0.1875 to 0.1875
Outputs:
- pooled_grad: bfloat16 [28, 128, 4096], P('table', None, 'copy')
- grad_first: bfloat16 [16, 3328, 4096], P('copy', None, 'table')
- grad_bias: float32 [16, 4096], P('copy', 'table')
- grad_head: float32 [16, 4096], P('copy', 'table')
- loss_mean: float32 [16], P('copy')
The draws below stay inside these ranges and needn't reach their ends.
Inputs may be any that keep to these rules, and one draw needn't show every extreme that they name: The slots are distinct; table t lies on the device of index slot_of_table[t] // 14 of the table axis; slots 0 and 27 are always used. A pairing: partner[partner[c]] == c and partner[c] != c.
All inputs are finite; a program needn't handle non-finite values. No bound on the sum of `labels` on one device may be relied on, other than what follows from the above.
Results may differ from the reference program's by a relative error of at most 0.017.
Values may be sent and summed in bfloat16 or wider, within the bound.
No kernel may reach another device: no remote copies, remote signals or barrier semaphores. Data moves between devices by JAX's collectives and lax.ppermute only.
A program may use at most 192 MiB of HBM per device.

```python
import jax
import jax.numpy as jnp
from jax import lax

TABLES = 26
EMB = 128
H1 = 4096
GROUP_ROWS = 256
COPIES = 16
FEATURES = 3328
SLOTS = 28
ROWS = 4096
N_TABLE = 2


def draw_slot_of_table(key, part):
    key = jax.random.fold_in(key, 11)
    first_key, second_key = jax.random.split(key)
    middle = jax.random.permutation(first_key, jnp.arange(1, SLOTS - 1, dtype=jnp.int32))
    chosen = jnp.concatenate([jnp.array([0, SLOTS - 1], dtype=jnp.int32), middle[:TABLES - 2]])
    return jax.random.permutation(second_key, chosen)


def draw_partner(key, part):
    key = jax.random.fold_in(key, 23)
    ordering = jax.random.permutation(key, jnp.arange(COPIES, dtype=jnp.int32))
    positions = jnp.arange(COPIES, dtype=jnp.int32)
    mates = ordering[jnp.bitwise_xor(positions, 1)]
    return jnp.zeros((COPIES,), jnp.int32).at[ordering].set(mates)


def with_ends(result, own_key, least, top_value):
    longest = result.shape.index(max(result.shape))
    spots = []
    for shift in (0, 1):
        where = [jax.random.randint(jax.random.fold_in(own_key, axis), (), 0, length) for axis, length in enumerate(result.shape)]
        where[longest] = (where[longest] + shift) % result.shape[longest]
        spots.append(tuple(where))
    return result.at[spots[0]].set(least).at[spots[1]].set(top_value)


def steps_of(rng, extent, cuts, low, top_value):
    gain, own = 1.0, jax.random.fold_in(rng, 6)
    for dim, shards_of in cuts:
        steps = jnp.exp(jax.random.uniform(jax.random.fold_in(own, dim), (shards_of,), jnp.float32, low / len(cuts), top_value / len(cuts)))
        gain = gain * jnp.repeat(steps, extent[dim] // shards_of).reshape([-1 if axis == dim else 1 for axis in range(len(extent))])
    return gain


def centred(key, shape, width, reach, pieces=(), held_as=jnp.bfloat16):
    gain = steps_of(key, shape, pieces, -0.22, 0.18) if pieces else 1.0
    result = jax.random.normal(key, shape, jnp.float32) * width * gain
    return jnp.minimum(jnp.maximum(result, -reach), reach).astype(held_as)


def setup_inputs(seed: int = 0) -> dict:
    keys = jax.random.split(jax.random.key(seed), 8)
    return {
        "pooled": centred(keys[0], (ROWS, SLOTS, EMB), 1.0, 6.0, ((0, 16), (1, 2))),
        "slot_of_table": draw_slot_of_table(jax.random.fold_in(keys[7], 71), 0),
        "partner": draw_partner(jax.random.fold_in(keys[7], 71), 0),
        "labels": with_ends((jax.random.randint(keys[3], (ROWS,), 0, 4) < 1).astype(jnp.int32), jax.random.fold_in(keys[3], 1), 0, 1),
        "w_first": centred(keys[4], (COPIES, FEATURES, H1), FEATURES ** -0.5, 0.109375, ((0, 16), (2, 2))),
        "b_first": centred(keys[5], (COPIES, H1), 0.5, 3.0, ((0, 16), (1, 2))),
        "w_head": centred(keys[6], (COPIES, H1), (H1 // 4) ** -0.5, 0.1875, ((0, 16), (1, 2))),
    }


def swish_parts(pre_value):
    sigmoid_v = jax.nn.sigmoid(pre_value)
    return pre_value * sigmoid_v, sigmoid_v * (1.0 + pre_value * (1.0 - sigmoid_v))


def one_copy(pooled_copy, slot_of_table, labels_copy, w_own, b_own, h_own, w_peer, b_peer, h_peer):
    row_count = pooled_copy.shape[0]
    features = jnp.take(pooled_copy, slot_of_table, axis=1).reshape(row_count, -1)
    student_pre = jnp.dot(features, w_own, preferred_element_type=jnp.float32) + b_own.astype(jnp.float32)
    teacher_pre = jnp.dot(features, w_peer, preferred_element_type=jnp.float32) + b_peer.astype(jnp.float32)
    activation, derivative = swish_parts(student_pre)
    teacher_act, unused_slope = swish_parts(teacher_pre)
    student_logit = jnp.sum(activation * h_own.astype(jnp.float32)[None, :], axis=1)
    teacher_logit = jnp.sum(teacher_act * h_peer.astype(jnp.float32)[None, :], axis=1)
    targets = labels_copy.astype(jnp.float32)
    soft_target = jax.nn.sigmoid(teacher_logit)
    loss_mean = jnp.mean(2.0 * jax.nn.softplus(student_logit) - targets * student_logit - soft_target * student_logit)
    logit_grad = 2.0 * jax.nn.sigmoid(student_logit) - targets - soft_target
    grad_pre = logit_grad[:, None] * h_own.astype(jnp.float32)[None, :] * derivative
    grad_low = grad_pre.astype(jnp.bfloat16)
    grad_first = lax.dot_general(features, grad_low, (((0,), (0,)), ((), ())), preferred_element_type=jnp.float32).astype(jnp.bfloat16)
    grad_bias = jnp.sum(grad_pre, axis=0)
    grad_head = jnp.sum(logit_grad[:, None] * activation, axis=0)
    unit_width = w_own.shape[1] // N_TABLE
    summed = jnp.zeros((row_count, SLOTS, EMB), jnp.float32)
    for block_index in range(N_TABLE):
        lower = block_index * unit_width
        partial_value = lax.dot_general(grad_low[:, lower:lower + unit_width], w_own[:, lower:lower + unit_width], (((1,), (1,)), ((), ())), preferred_element_type=jnp.float32)
        partial_value = lax.optimization_barrier(partial_value.astype(jnp.bfloat16)).astype(jnp.float32)
        placed = jnp.zeros((row_count, SLOTS, EMB), jnp.float32).at[:, slot_of_table, :].add(partial_value.reshape(row_count, TABLES, EMB))
        summed = summed + placed
    pooled_grad = jnp.transpose(summed, (1, 2, 0)).astype(jnp.bfloat16)
    return pooled_grad, grad_first, grad_bias, grad_head, loss_mean


def reference(pooled, slot_of_table, partner, labels, w_first, b_first, w_head):
    pooled_copies = pooled.reshape(COPIES, GROUP_ROWS, SLOTS, EMB)
    label_copies = labels.reshape(COPIES, GROUP_ROWS)

    def per_copy(copy_index):
        peer_index = partner[copy_index]
        return one_copy(pooled_copies[copy_index], slot_of_table, label_copies[copy_index], w_first[copy_index], b_first[copy_index], w_head[copy_index], w_first[peer_index], b_first[peer_index], w_head[peer_index])

    results = lax.map(per_copy, jnp.arange(COPIES, dtype=jnp.int32))
    pooled_grad = jnp.transpose(results[0], (1, 2, 0, 3)).reshape(SLOTS, EMB, ROWS)
    return pooled_grad, results[1], results[2], results[3], results[4]
```

```python
import functools

import jax
import jax.numpy as jnp
from jax import lax
from jax.experimental import pallas as pl
from jax.experimental.pallas import tpu as pltpu
from jax.sharding import PartitionSpec as P

VMEM_LIMIT = 52 * 1024 * 1024


def whole(shape):
    return pl.BlockSpec(shape, lambda *_: (0,) * len(shape))


def tile_of(width):
    return 256 if width % 256 == 0 else width


def params():
    return pltpu.CompilerParams(
        dimension_semantics=("arbitrary",), vmem_limit_bytes=VMEM_LIMIT
    )


def copy_features(where, blocks, feats):
    slots, _, emb = blocks[0].shape
    for t in range(feats.shape[1] // emb):
        place = where[t]
        for k, block in enumerate(blocks):

            @pl.when(place // slots == k)
            def _():
                feats[:, t * emb : (t + 1) * emb] = block[place - k * slots]


def row_sum(wide):
    total = wide[:, :128]
    for start in range(128, wide.shape[1], 128):
        total = total + wide[:, start : start + 128]
    return jnp.sum(total.T, axis=0, keepdims=True)


def forward_body(student, count, where, *refs):
    blocks, (w, b, h) = refs[:count], refs[count : count + 3]
    if student:
        logit, slope, active, feats = refs[count + 3 :]
    else:
        logit, feats = refs[count + 3 :]
    step = pl.program_id(0)

    @pl.when(step == 0)
    def _():
        copy_features(where, blocks, feats)
        logit[...] = jnp.zeros_like(logit)

    pre = jnp.dot(feats[...], w[...], preferred_element_type=jnp.float32)
    pre = pre + b[...].astype(jnp.float32)
    head = h[...].astype(jnp.float32)
    sigmoid = jax.nn.sigmoid(pre)
    act = pre * sigmoid
    logit[...] += row_sum(act * head)
    if student:
        slope[...] = (head * (sigmoid * (1.0 + pre * (1.0 - sigmoid)))).astype(jnp.bfloat16)
        active[...] = act.astype(jnp.bfloat16)


def forward(student, where, blocks, w, b, h):
    slots, rows, emb = blocks[0].shape
    depth, units = w.shape
    tile = tile_of(units)
    column = lambda i, *_: (0, i)
    out_shape = [jax.ShapeDtypeStruct((1, rows), jnp.float32)]
    out_specs = [whole((1, rows))]
    if student:
        out_shape += [jax.ShapeDtypeStruct((rows, units), jnp.bfloat16)] * 2
        out_specs += [pl.BlockSpec((rows, tile), column)] * 2
    return pl.pallas_call(
        functools.partial(forward_body, student, len(blocks)),
        grid_spec=pltpu.PrefetchScalarGridSpec(
            num_scalar_prefetch=1,
            grid=(units // tile,),
            in_specs=[whole(blocks[0].shape)] * len(blocks)
            + [
                pl.BlockSpec((depth, tile), column),
                pl.BlockSpec((1, tile), column),
                pl.BlockSpec((1, tile), column),
            ],
            out_specs=out_specs,
            scratch_shapes=[pltpu.VMEM((rows, depth), jnp.bfloat16)],
        ),
        out_shape=out_shape,
        compiler_params=params(),
        cost_estimate=pl.CostEstimate(
            flops=2 * rows * depth * units,
            bytes_accessed=2 * depth * units + 4 * rows * units,
            transcendentals=rows * units,
        ),
    )(where, *blocks, w, b, h)


def turn_body(count, where, *refs):
    blocks, out = refs[:count], refs[count]
    slots, _, emb = blocks[0].shape
    for t in range(out.shape[0] // emb):
        place = where[t]
        for k, block in enumerate(blocks):

            @pl.when(place // slots == k)
            def _():
                out[t * emb : (t + 1) * emb, :] = block[place - k * slots].T


def turned_features(where, blocks):
    slots, rows, emb = blocks[0].shape
    depth = where.shape[0] * emb
    return pl.pallas_call(
        functools.partial(turn_body, len(blocks)),
        grid_spec=pltpu.PrefetchScalarGridSpec(
            num_scalar_prefetch=1,
            grid=(1,),
            in_specs=[whole(blocks[0].shape)] * len(blocks),
            out_specs=whole((depth, rows)),
        ),
        out_shape=jax.ShapeDtypeStruct((depth, rows), jnp.bfloat16),
        compiler_params=params(),
        cost_estimate=pl.CostEstimate(
            flops=depth * rows, bytes_accessed=4 * depth * rows, transcendentals=0
        ),
    )(where, *blocks)


def slots_body(table_at, slope, w, out, held, arrived):
    slots, emb, rows = out.shape

    def fetch(j):
        start = pl.multiple_of(jnp.maximum(table_at[j], 0) * emb, emb)
        return pltpu.make_async_copy(
            w.at[pl.ds(start, emb), :], held.at[pl.ds(j * emb, emb), :], arrived.at[j]
        )

    for j in range(slots):
        fetch(j).start()
    group = 7 if slots % 7 == 0 else slots
    for first in range(0, slots, group):
        for j in range(first, first + group):
            fetch(j).wait()
        value = lax.dot_general(
            held[first * emb : (first + group) * emb, :],
            slope[...],
            (((1,), (1,)), ((), ())),
            preferred_element_type=jnp.float32,
        )
        for j in range(first, first + group):
            part = value[(j - first) * emb : (j - first + 1) * emb, :]
            used = (table_at[j] >= 0).astype(jnp.float32)
            out[j] = (part * used).astype(jnp.bfloat16)


def slot_grads(table_at, slope, w, emb):
    slots = table_at.shape[0]
    rows, units = slope.shape
    return pl.pallas_call(
        slots_body,
        grid_spec=pltpu.PrefetchScalarGridSpec(
            num_scalar_prefetch=1,
            grid=(1,),
            in_specs=[whole((rows, units)), pl.BlockSpec(memory_space=pl.ANY)],
            out_specs=whole((slots, emb, rows)),
            scratch_shapes=[
                pltpu.VMEM((slots * emb, units), jnp.bfloat16),
                pltpu.SemaphoreType.DMA((slots,)),
            ],
        ),
        out_shape=jax.ShapeDtypeStruct((slots, emb, rows), jnp.bfloat16),
        compiler_params=params(),
        cost_estimate=pl.CostEstimate(
            flops=2 * rows * slots * emb * units,
            bytes_accessed=2 * slots * emb * units,
            transcendentals=0,
        ),
    )(table_at, slope, w)


def first_body(z_ref, t_ref, y_ref, turned, slope, active, grad, bias, head, loss, scale, column):
    step = pl.program_id(0)
    rows = z_ref.shape[1]

    @pl.when(step == 0)
    def _():
        z = jnp.sum(z_ref[...], axis=0, keepdims=True)
        soft = jax.nn.sigmoid(jnp.sum(t_ref[...], axis=0, keepdims=True))
        y = y_ref[...].astype(jnp.float32)
        grads = 2.0 * jax.nn.sigmoid(z) - y - soft
        scale[...] = grads
        softplus = jnp.maximum(z, 0.0) + jnp.log1p(jnp.exp(-jnp.abs(z)))
        losses = 2.0 * softplus - y * z - soft * z
        loss[...] = jnp.sum(losses, axis=1, keepdims=True) / rows
        column[...] = jnp.broadcast_to(grads, (column.shape[1], rows)).T

    by_row = jnp.concatenate([column[...]] * (slope.shape[1] // column.shape[1]), axis=1)
    pre = slope[...].astype(jnp.float32) * by_row
    bias[...] = jnp.sum(pre, axis=0, keepdims=True)
    head[...] = jnp.sum(active[...].astype(jnp.float32) * by_row, axis=0, keepdims=True)
    grad[...] = jnp.dot(
        turned[...], pre.astype(jnp.bfloat16), preferred_element_type=jnp.float32
    ).astype(jnp.bfloat16)


def first_grads(z_parts, t_parts, labels, turned, slope, active):
    depth, rows = turned.shape
    units = slope.shape[1]
    tile = tile_of(units)
    column = lambda i: (0, i)
    return pl.pallas_call(
        first_body,
        grid=(units // tile,),
        in_specs=[
            whole(z_parts.shape),
            whole(t_parts.shape),
            whole(labels.shape),
            whole((depth, rows)),
            pl.BlockSpec((rows, tile), column),
            pl.BlockSpec((rows, tile), column),
        ],
        out_specs=[
            pl.BlockSpec((depth, tile), column),
            pl.BlockSpec((1, tile), column),
            pl.BlockSpec((1, tile), column),
            whole((1, 1)),
            whole((1, rows)),
        ],
        out_shape=[
            jax.ShapeDtypeStruct((depth, units), jnp.bfloat16),
            jax.ShapeDtypeStruct((1, units), jnp.float32),
            jax.ShapeDtypeStruct((1, units), jnp.float32),
            jax.ShapeDtypeStruct((1, 1), jnp.float32),
            jax.ShapeDtypeStruct((1, rows), jnp.float32),
        ],
        scratch_shapes=[pltpu.VMEM((rows, 128), jnp.float32)],
        compiler_params=params(),
        cost_estimate=pl.CostEstimate(
            flops=2 * rows * depth * units, bytes_accessed=2 * depth * units, transcendentals=0
        ),
    )(z_parts, t_parts, labels, turned, slope, active)


def across(value, shift):
    count = lax.axis_size("table")
    return lax.ppermute(value, "table", [(i, (i + shift) % count) for i in range(count)])


def from_partner(value, distance, shifts=(0,)):
    copies, tables = lax.axis_size("copy"), lax.axis_size("table")

    def swap(bits):
        def run(given):
            return tuple(
                lax.ppermute(
                    given,
                    ("copy", "table"),
                    [
                        (c * tables + i, (c ^ bits) * tables + (i + shift) % tables)
                        for c in range(copies)
                        for i in range(tables)
                    ],
                )
                for shift in shifts
            )

        return run

    return lax.switch(distance - 1, [swap(bits) for bits in range(1, copies)], value)


def on_device(pooled, slot_of_table, partner, labels, w_first, b_first, w_head):
    tables = lax.axis_size("table")
    rows, slots, emb = pooled.shape
    w = w_first[0]
    me_copy, me_table = lax.axis_index("copy"), lax.axis_index("table")
    distance = jnp.bitwise_xor(me_copy, partner[me_copy])

    owner = slot_of_table // slots
    where = (me_table - owner) % tables * slots + slot_of_table % slots
    target = (owner - me_table) % tables * slots + slot_of_table % slots
    hit = jnp.arange(tables * slots, dtype=jnp.int32)[:, None] == target[None, :]
    numbers = jnp.arange(1, slot_of_table.shape[0] + 1, dtype=jnp.int32)
    table_at = jnp.sum(jnp.where(hit, numbers[None, :], 0), axis=1) - 1

    own = jnp.transpose(pooled, (1, 0, 2))
    blocks = [own] + [across(own, k) for k in range(1, tables)]
    (theirs,) = from_partner(own, distance)
    their_blocks = [theirs] + [across(theirs, k) for k in range(1, tables)]

    z_own, slope, active = forward(True, where, blocks, w, b_first, w_head)
    sent = [
        across(slot_grads(table_at[k * slots : (k + 1) * slots], slope, w, emb), k)
        for k in range(1, tables)
    ]
    kept = slot_grads(table_at[:slots], slope, w, emb)
    turned = turned_features(where, blocks)
    z_parts = jnp.concatenate([z_own] + [across(z_own, k) for k in range(1, tables)], axis=0)

    (t_own,) = forward(False, where, their_blocks, w, b_first, w_head)
    t_parts = jnp.concatenate(from_partner(t_own, distance, tuple(range(tables))), axis=0)

    grad_first, grad_bias, grad_head, loss, scale = first_grads(
        z_parts, t_parts, labels.reshape(1, rows), turned, slope, active
    )
    total = kept.astype(jnp.float32)
    for part in sent:
        total = total + part.astype(jnp.float32)
    pooled_grad = (total * scale[None]).astype(jnp.bfloat16)
    return (pooled_grad, grad_first[None], grad_bias, grad_head, loss.reshape(1))


def solution(mesh):
    in_specs = (
        P("copy", "table", None),
        P(),
        P(),
        P("copy"),
        P("copy", None, "table"),
        P("copy", "table"),
        P("copy", "table"),
    )
    out_specs = (
        P("table", None, "copy"),
        P("copy", None, "table"),
        P("copy", "table"),
        P("copy", "table"),
        P("copy"),
    )
    return jax.shard_map(
        on_device, mesh=mesh, in_specs=in_specs, out_specs=out_specs, check_vma=False
    )
```

```python
import functools

import jax
import jax.numpy as jnp
from jax import lax
from jax.experimental import pallas as pl
from jax.experimental.pallas import tpu as pltpu
from jax.sharding import PartitionSpec as P

VMEM_LIMIT = 24 * 1024 * 1024
VMEM = pl.BlockSpec(memory_space=pltpu.VMEM)
SMEM = pl.BlockSpec(memory_space=pltpu.SMEM)
HBM = pl.BlockSpec(memory_space=pltpu.HBM)
TILE = 256


def whole(shape):
    return pl.BlockSpec(shape, lambda *_: (0,) * len(shape))


def tiles(width):
    return TILE if width % TILE == 0 else width


def part_of(i, size):
    return pl.ds(pl.multiple_of(i * size, size), size)


def copy_features(where, blocks, feats):
    slots, _, emb = blocks[0].shape

    @pl.loop(0, feats.shape[1] // emb)
    def _(t):
        place = where[t]
        for k, block in enumerate(blocks):

            @pl.when(place // slots == k)
            def _():
                feats[:, part_of(t, emb)] = block[place - k * slots]


def forward_tiles(feats, w, b, held, finish, arrive=lambda i: None):
    tile = held.shape[1]
    count = w.shape[1] // tile

    def product(i):
        arrive(i)
        cut = part_of(i, tile)
        value = jnp.dot(feats[...], w[:, cut], preferred_element_type=jnp.float32)
        return value + b[:, cut].astype(jnp.float32)

    held[...] = product(0)

    @pl.loop(1, count)
    def _(i):
        before = held[...]
        value = product(i)
        finish(i - 1, before)
        held[...] = value

    finish(count - 1, held[...])


def swish(pre):
    sigmoid = 0.5 * jnp.tanh(0.5 * pre) + 0.5
    return sigmoid, pre * sigmoid


def add_lanes(total, wide):
    for lane in range(0, wide.shape[1], 128):
        total[...] += wide[:, lane : lane + 128]


def student_body(count, where, target, *refs):
    given, others, refs = refs[:4], refs[4 : 3 + count], refs[3 + count :]
    logit, slope, active, feats, w, *refs = refs
    grads, (held, total, turned, own, b, h, here, arrived) = refs[:count], refs[count:]
    slots, emb, _ = grads[0].shape
    tile = held.shape[1]
    small = [
        pltpu.make_async_copy(source, here_now, here.at[i])
        for i, (source, here_now) in enumerate(zip(given[1:], (own, b, h)))
    ]
    for copy in small:
        copy.start()

    def fetch(i):
        cut = part_of(i, tile)
        return pltpu.make_async_copy(given[0].at[:, cut], w.at[:, cut], arrived.at[i])

    @pl.loop(0, w.shape[1] // tile)
    def _(i):
        fetch(i).start()

    for copy in small:
        copy.wait()
    copy_features(where, [own, *others], feats)
    total[...] = jnp.zeros_like(total)

    def finish(i, pre):
        cut = part_of(i, pre.shape[1])
        head = h[:, cut].astype(jnp.float32)
        sigmoid, act = swish(pre)
        add_lanes(total, act * head)
        low = (head * (sigmoid + act * (1.0 - sigmoid))).astype(jnp.bfloat16)
        slope[:, cut] = low
        turned[cut, :] = low.T
        active[:, cut] = act.astype(jnp.bfloat16)

    forward_tiles(feats, w, b, held, finish, lambda i: fetch(i).wait())
    logit[...] = jnp.sum(total[...].T, axis=0, keepdims=True)

    for grad in grads:
        grad[...] = jnp.zeros_like(grad)

    @pl.loop(0, w.shape[0] // (2 * emb))
    def _(i):
        value = jnp.dot(
            w[part_of(i, 2 * emb), :], turned[...], preferred_element_type=jnp.float32
        ).astype(jnp.bfloat16)
        for half in range(2):
            place = target[2 * i + half]
            for k, grad in enumerate(grads):

                @pl.when(place // slots == k)
                def _():
                    grad[place - k * slots] = value[half * emb : (half + 1) * emb, :]


def student(where, target, blocks, w, b, h):
    slots, rows, emb = blocks[0].shape
    depth, units = w.shape
    count = len(blocks)
    shape = jax.ShapeDtypeStruct
    return pl.pallas_call(
        functools.partial(student_body, count),
        in_specs=[SMEM, SMEM] + [HBM] * 4 + [VMEM] * (count - 1),
        out_specs=[VMEM] * (5 + count),
        out_shape=[
            shape((1, rows), jnp.float32),
            shape((rows, units), jnp.bfloat16),
            shape((rows, units), jnp.bfloat16),
            shape((rows, depth), jnp.bfloat16),
            shape((depth, units), jnp.bfloat16),
        ]
        + [shape((slots, emb, rows), jnp.bfloat16)] * count,
        scratch_shapes=[
            pltpu.VMEM((rows, tiles(units)), jnp.float32),
            pltpu.VMEM((rows, 128), jnp.float32),
            pltpu.VMEM((units, rows), jnp.bfloat16),
            pltpu.VMEM((slots, rows, emb), jnp.bfloat16),
            pltpu.VMEM((1, units), jnp.bfloat16),
            pltpu.VMEM((1, units), jnp.bfloat16),
            pltpu.SemaphoreType.DMA((3,)),
            pltpu.SemaphoreType.DMA((units // tiles(units),)),
        ],
        compiler_params=pltpu.CompilerParams(vmem_limit_bytes=VMEM_LIMIT),
        cost_estimate=pl.CostEstimate(
            flops=4 * rows * depth * units,
            bytes_accessed=2 * depth * units,
            transcendentals=rows * units,
        ),
    )(where, target, w, blocks[0], b, h, *blocks[1:])


def teacher_body(count, where, *refs):
    blocks, (w, b, h, logit, feats, held, total) = refs[:count], refs[count:]
    copy_features(where, blocks, feats)
    total[...] = jnp.zeros_like(total)

    def finish(i, pre):
        head = h[:, part_of(i, pre.shape[1])].astype(jnp.float32)
        add_lanes(total, swish(pre)[1] * head)

    forward_tiles(feats, w, b, held, finish)
    logit[...] = jnp.sum(total[...].T, axis=0, keepdims=True)


def teacher(where, blocks, w, b, h):
    _, rows, _ = blocks[0].shape
    depth, units = w.shape
    count = len(blocks)
    return pl.pallas_call(
        functools.partial(teacher_body, count),
        in_specs=[SMEM] + [VMEM] * (count + 3),
        out_specs=VMEM,
        out_shape=jax.ShapeDtypeStruct((1, rows), jnp.float32),
        scratch_shapes=[
            pltpu.VMEM((rows, depth), jnp.bfloat16),
            pltpu.VMEM((rows, tiles(units)), jnp.float32),
            pltpu.VMEM((rows, 128), jnp.float32),
        ],
        compiler_params=pltpu.CompilerParams(vmem_limit_bytes=VMEM_LIMIT),
        cost_estimate=pl.CostEstimate(
            flops=2 * rows * depth * units,
            bytes_accessed=2 * depth * units,
            transcendentals=rows * units,
        ),
    )(where, *blocks, w, b, h)


def first_body(count, y_ref, *refs):
    zs, ts, refs = refs[:count], refs[count : 2 * count], refs[2 * count :]
    feats, slope, active, grad, bias, head, loss, scale, low, ready, sent = refs
    rows = y_ref.shape[1]
    z = sum(ref[...] for ref in zs)
    soft = jax.nn.sigmoid(sum(ref[...] for ref in ts))
    y = y_ref[...].astype(jnp.float32)
    grads = 2.0 * jax.nn.sigmoid(z) - y - soft
    scale[...] = grads
    softplus = jnp.maximum(z, 0.0) + jnp.log1p(jnp.exp(-jnp.abs(z)))
    losses = 2.0 * softplus - y * z - soft * z
    loss[...] = jnp.sum(losses, axis=1, keepdims=True) / rows
    column = jnp.broadcast_to(grads, (128, rows)).T

    @pl.loop(0, slope.shape[1] // 128)
    def _(i):
        cut = part_of(i, 128)
        pre = slope[:, cut].astype(jnp.float32) * column
        low[:, cut] = pre.astype(jnp.bfloat16)
        bias[:, cut] = jnp.sum(pre, axis=0, keepdims=True)
        head[:, cut] = jnp.sum(
            active[:, cut].astype(jnp.float32) * column, axis=0, keepdims=True
        )

    part = ready.shape[1]
    steps = grad.shape[0] // part

    def send(i, slot):
        return pltpu.make_async_copy(
            ready.at[slot], grad.at[part_of(i, part), :], sent.at[slot]
        )

    @pl.loop(0, steps)
    def _(i):
        slot = i % 2

        @pl.when(i >= 2)
        def _():
            send(i - 2, slot).wait()

        ready[slot] = lax.dot_general(
            feats[:, part_of(i, part)],
            low[...],
            (((0,), (0,)), ((), ())),
            preferred_element_type=jnp.float32,
        ).astype(jnp.bfloat16)
        send(i, slot).start()

    for i in range(max(steps - 2, 0), steps):
        send(i, i % 2).wait()


def first_grads(z_parts, t_parts, labels, feats, slope, active):
    rows, depth = feats.shape
    units = slope.shape[1]
    shape = jax.ShapeDtypeStruct
    return pl.pallas_call(
        functools.partial(first_body, len(z_parts)),
        in_specs=[VMEM] * (4 + len(z_parts) + len(t_parts)),
        out_specs=[HBM] + [VMEM] * 4,
        out_shape=[
            shape((depth, units), jnp.bfloat16),
            shape((1, units), jnp.float32),
            shape((1, units), jnp.float32),
            shape((1, 1), jnp.float32),
            shape((1, rows), jnp.float32),
        ],
        scratch_shapes=[
            pltpu.VMEM((rows, units), jnp.bfloat16),
            pltpu.VMEM((2, tiles(depth), units), jnp.bfloat16),
            pltpu.SemaphoreType.DMA((2,)),
        ],
        compiler_params=pltpu.CompilerParams(vmem_limit_bytes=VMEM_LIMIT),
        cost_estimate=pl.CostEstimate(
            flops=2 * rows * depth * units, bytes_accessed=2 * depth * units, transcendentals=0
        ),
    )(labels, *z_parts, *t_parts, feats, slope, active)


def scaled_body(count, scale, *refs):
    total = sum(ref[...].astype(jnp.float32) for ref in refs[:count])
    refs[count][...] = (total * scale[...]).astype(jnp.bfloat16)


def scaled_sum(scale, parts):
    slots, emb, rows = parts[0].shape
    group = 7 if slots % 7 == 0 else slots
    block = pl.BlockSpec((group, emb, rows), lambda i: (i, 0, 0))
    return pl.pallas_call(
        functools.partial(scaled_body, len(parts)),
        grid=(slots // group,),
        in_specs=[whole((1, 1, rows))] + [block] * len(parts),
        out_specs=block,
        out_shape=jax.ShapeDtypeStruct((slots, emb, rows), jnp.bfloat16),
        compiler_params=pltpu.CompilerParams(vmem_limit_bytes=VMEM_LIMIT),
    )(scale.reshape(1, 1, rows), *parts)


def across(value, shift):
    count = lax.axis_size("table")
    return lax.ppermute(value, "table", [(i, (i + shift) % count) for i in range(count)])


def swap(bits, value, shifts):
    copies, tables = lax.axis_size("copy"), lax.axis_size("table")
    return tuple(
        lax.ppermute(
            value,
            ("copy", "table"),
            [
                (c * tables + i, (c ^ bits) * tables + (i + shift) % tables)
                for c in range(copies)
                for i in range(tables)
            ],
        )
        for shift in shifts
    )


def after(value, other):
    return lax.optimization_barrier((value, other))[0]


def from_partner(value, distance, shifts):
    branches = [
        lambda given, bits=bits: swap(bits, given, shifts)
        for bits in range(1, lax.axis_size("copy"))
    ]
    return lax.switch(distance - 1, branches, value)


def on_device(pooled, slot_of_table, partner, labels, w_first, b_first, w_head):
    tables = lax.axis_size("table")
    rows, slots, emb = pooled.shape
    me_copy, me_table = lax.axis_index("copy"), lax.axis_index("table")
    distance = jnp.bitwise_xor(me_copy, partner[me_copy])

    owner = slot_of_table // slots
    where = (me_table - owner) % tables * slots + slot_of_table % slots
    target = (owner - me_table) % tables * slots + slot_of_table % slots

    own = jnp.transpose(pooled, (1, 0, 2))
    blocks = [own] + [across(own, k) for k in range(1, tables)]
    pieces = 2 if slots % 2 == 0 else 1
    size = slots // pieces
    theirs = []
    for i in range(pieces):
        piece = own[i * size : (i + 1) * size]
        if theirs:
            piece = after(piece, theirs[-1])
        theirs += from_partner(piece, distance, (0,))
    their_blocks = list(theirs)
    for k in range(1, tables):
        their_blocks += [across(piece, k) for piece in theirs]

    z_own, slope, active, feats, w, *parts = student(
        where, target, blocks, w_first[0], b_first, w_head
    )
    parts = parts[:1] + [across(part, k) for k, part in enumerate(parts) if k]
    z_parts = [z_own] + [across(z_own, k) for k in range(1, tables)]

    t_own = teacher(where, their_blocks, w, b_first, w_head)
    t_parts = from_partner(t_own, distance, tuple(range(tables)))

    grad_first, grad_bias, grad_head, loss, scale = first_grads(
        z_parts, t_parts, labels.reshape(1, rows), feats, slope, active
    )
    pooled_grad = scaled_sum(scale, parts)
    return (pooled_grad, grad_first[None], grad_bias, grad_head, loss.reshape(1))


def solution(mesh):
    in_specs = (
        P("copy", "table", None),
        P(),
        P(),
        P("copy"),
        P("copy", None, "table"),
        P("copy", "table"),
        P("copy", "table"),
    )
    out_specs = (
        P("table", None, "copy"),
        P("copy", None, "table"),
        P("copy", "table"),
        P("copy", "table"),
        P("copy"),
    )
    return jax.shard_map(
        on_device, mesh=mesh, in_specs=in_specs, out_specs=out_specs, check_vma=False
    )
```

```python
import functools

import jax
import jax.numpy as jnp
from jax import lax
from jax.experimental import pallas as pl
from jax.experimental.pallas import tpu as pltpu
from jax.sharding import PartitionSpec as P

VMEM_LIMIT = 24 * 1024 * 1024
VMEM = pl.BlockSpec(memory_space=pltpu.VMEM)
SMEM = pl.BlockSpec(memory_space=pltpu.SMEM)
HBM = pl.BlockSpec(memory_space=pltpu.HBM)
TILE = 256


def in_hbm(value):
    return pltpu.with_memory_space_constraint(value, pltpu.HBM)


def whole(shape):
    return pl.BlockSpec(shape, lambda *_: (0,) * len(shape))


def tiles(width):
    return TILE if width % TILE == 0 else width


def part_of(i, size):
    return pl.ds(pl.multiple_of(i * size, size), size)


def copy_features(slot_of, blocks, feats):
    me, tables = lax.axis_index("table"), lax.axis_size("table")
    emb = blocks[0][0].shape[2]
    slots = sum(piece.shape[0] for piece in blocks[0])

    @pl.loop(0, feats.shape[1] // emb)
    def _(t):
        slot = slot_of[t]
        place = lax.rem(slot, slots)
        group = lax.rem(me + tables - slot // slots, tables)
        for k, pieces in enumerate(blocks):
            first = 0
            for piece in pieces:
                last = first + piece.shape[0]

                @pl.when((group == k) & (place >= first) & (place < last))
                def _():
                    feats[:, part_of(t, emb)] = piece[place - first]

                first = last


def forward_tiles(feats, w, b, held, finish, arrive=lambda i: None):
    tile = held.shape[1]
    count = w.shape[1] // tile

    def product(i):
        arrive(i)
        cut = part_of(i, tile)
        value = jnp.dot(feats[...], w[:, cut], preferred_element_type=jnp.float32)
        return value + b[:, cut].astype(jnp.float32)

    held[...] = product(0)

    @pl.loop(1, count)
    def _(i):
        before = held[...]
        value = product(i)
        finish(i - 1, before)
        held[...] = value

    finish(count - 1, held[...])


def swish(pre):
    sigmoid = 0.5 * jnp.tanh(0.5 * pre) + 0.5
    return sigmoid, pre * sigmoid


def add_lanes(total, wide):
    for lane in range(0, wide.shape[1], 128):
        total[...] += wide[:, lane : lane + 128]


def student_body(count, slot_of, *refs):
    given, others, refs = refs[:4], refs[4 : 3 + count], refs[3 + count :]
    logit, slope, active, feats, w, *refs = refs
    grads, (held, total, turned, own, b, h, here, arrived) = refs[:count], refs[count:]
    slots, emb, _ = grads[0].shape
    tile = held.shape[1]
    small = [
        pltpu.make_async_copy(source, here_now, here.at[i])
        for i, (source, here_now) in enumerate(zip(given[1:], (own, b, h)))
    ]
    for copy in small:
        copy.start()

    def fetch(i):
        cut = part_of(i, tile)
        return pltpu.make_async_copy(given[0].at[:, cut], w.at[:, cut], arrived.at[i])

    @pl.loop(0, w.shape[1] // tile)
    def _(i):
        fetch(i).start()

    for copy in small:
        copy.wait()
    copy_features(slot_of, [[own]] + [[other] for other in others], feats)
    total[...] = jnp.zeros_like(total)

    def finish(i, pre):
        cut = part_of(i, pre.shape[1])
        head = h[:, cut].astype(jnp.float32)
        sigmoid, act = swish(pre)
        add_lanes(total, act * head)
        low = (head * (sigmoid + act * (1.0 - sigmoid))).astype(jnp.bfloat16)
        slope[:, cut] = low
        turned[cut, :] = low.T
        active[:, cut] = act.astype(jnp.bfloat16)

    forward_tiles(feats, w, b, held, finish, lambda i: fetch(i).wait())
    logit[...] = jnp.sum(total[...].T, axis=0, keepdims=True)

    for grad in grads:
        grad[...] = jnp.zeros_like(grad)

    me, tables = lax.axis_index("table"), lax.axis_size("table")
    used = w.shape[0] // emb
    group = max(n for n in range(1, 14) if used % n == 0)

    @pl.loop(0, used // group)
    def _(i):
        value = jnp.dot(
            w[part_of(i, group * emb), :], turned[...], preferred_element_type=jnp.float32
        ).astype(jnp.bfloat16)
        for j in range(group):
            slot = slot_of[group * i + j]
            owner = lax.rem(slot // slots + tables - me, tables)
            for k, grad in enumerate(grads):

                @pl.when(owner == k)
                def _():
                    grad[lax.rem(slot, slots)] = value[j * emb : (j + 1) * emb, :]


def student(slot_of, blocks, w, b, h):
    slots, rows, emb = blocks[0].shape
    depth, units = w.shape
    count = len(blocks)
    shape = jax.ShapeDtypeStruct
    return pl.pallas_call(
        functools.partial(student_body, count),
        in_specs=[SMEM] + [HBM] * 4 + [VMEM] * (count - 1),
        out_specs=[VMEM] * (5 + count),
        out_shape=[
            shape((1, rows), jnp.float32),
            shape((rows, units), jnp.bfloat16),
            shape((rows, units), jnp.bfloat16),
            shape((rows, depth), jnp.bfloat16),
            shape((depth, units), jnp.bfloat16),
        ]
        + [shape((slots, emb, rows), jnp.bfloat16)] * count,
        scratch_shapes=[
            pltpu.VMEM((rows, tiles(units)), jnp.float32),
            pltpu.VMEM((rows, 128), jnp.float32),
            pltpu.VMEM((units, rows), jnp.bfloat16),
            pltpu.VMEM((slots, rows, emb), jnp.bfloat16),
            pltpu.VMEM((1, units), jnp.bfloat16),
            pltpu.VMEM((1, units), jnp.bfloat16),
            pltpu.SemaphoreType.DMA((3,)),
            pltpu.SemaphoreType.DMA((units // tiles(units),)),
        ],
        compiler_params=pltpu.CompilerParams(vmem_limit_bytes=VMEM_LIMIT),
        cost_estimate=pl.CostEstimate(
            flops=4 * rows * depth * units,
            bytes_accessed=2 * depth * units,
            transcendentals=rows * units,
        ),
    )(slot_of, *(in_hbm(x) for x in (w, blocks[0], b, h)), *blocks[1:])


def teacher_body(pieces, slot_of, *refs):
    count = sum(pieces)
    blocks, (w, b, h, logit, feats, held, total) = list(refs[:count]), refs[count:]
    copy_features(slot_of, [[blocks.pop(0) for _ in range(n)] for n in pieces], feats)
    total[...] = jnp.zeros_like(total)

    def finish(i, pre):
        head = h[:, part_of(i, pre.shape[1])].astype(jnp.float32)
        add_lanes(total, swish(pre)[1] * head)

    forward_tiles(feats, w, b, held, finish)
    logit[...] = jnp.sum(total[...].T, axis=0, keepdims=True)


def teacher(slot_of, blocks, w, b, h):
    rows = blocks[0][0].shape[1]
    depth, units = w.shape
    pieces = [len(block) for block in blocks]
    count = sum(pieces)
    return pl.pallas_call(
        functools.partial(teacher_body, pieces),
        in_specs=[SMEM] + [VMEM] * (count + 3),
        out_specs=VMEM,
        out_shape=jax.ShapeDtypeStruct((1, rows), jnp.float32),
        scratch_shapes=[
            pltpu.VMEM((rows, depth), jnp.bfloat16),
            pltpu.VMEM((rows, tiles(units)), jnp.float32),
            pltpu.VMEM((rows, 128), jnp.float32),
        ],
        compiler_params=pltpu.CompilerParams(vmem_limit_bytes=VMEM_LIMIT),
        cost_estimate=pl.CostEstimate(
            flops=2 * rows * depth * units,
            bytes_accessed=2 * depth * units,
            transcendentals=rows * units,
        ),
    )(slot_of, *(piece for block in blocks for piece in block), w, b, h)


def rows_body(count, y_ref, *refs):
    zs, ts, refs = refs[:count], refs[count : 2 * count], refs[2 * count :]
    slope, active, low, bias, head, loss, scale = refs
    rows = y_ref.shape[1]
    z = sum(ref[...] for ref in zs)
    soft = jax.nn.sigmoid(sum(ref[...] for ref in ts))
    y = y_ref[...].astype(jnp.float32)
    grads = 2.0 * jax.nn.sigmoid(z) - y - soft
    scale[...] = grads
    softplus = jnp.maximum(z, 0.0) + jnp.log1p(jnp.exp(-jnp.abs(z)))
    losses = 2.0 * softplus - y * z - soft * z
    loss[...] = jnp.sum(losses, axis=1, keepdims=True) / rows
    column = jnp.broadcast_to(grads, (128, rows)).T

    @pl.loop(0, slope.shape[1] // 128)
    def _(i):
        cut = part_of(i, 128)
        pre = slope[:, cut].astype(jnp.float32) * column
        low[:, cut] = pre.astype(jnp.bfloat16)
        bias[:, cut] = jnp.sum(pre, axis=0, keepdims=True)
        head[:, cut] = jnp.sum(
            active[:, cut].astype(jnp.float32) * column, axis=0, keepdims=True
        )


def row_grads(z_parts, t_parts, labels, slope, active):
    rows, units = slope.shape
    shape = jax.ShapeDtypeStruct
    row, units_row = whole((1, rows)), whole((1, units))
    return pl.pallas_call(
        functools.partial(rows_body, len(z_parts)),
        grid=(1,),
        in_specs=[row] * (1 + len(z_parts) + len(t_parts)) + [VMEM] * 2,
        out_specs=[VMEM, units_row, units_row, whole((1, 1)), row],
        out_shape=[
            shape((rows, units), jnp.bfloat16),
            shape((1, units), jnp.float32),
            shape((1, units), jnp.float32),
            shape((1, 1), jnp.float32),
            shape((1, rows), jnp.float32),
        ],
        compiler_params=pltpu.CompilerParams(vmem_limit_bytes=VMEM_LIMIT),
    )(labels, *z_parts, *t_parts, slope, active)


def scaled_body(count, scale, *refs):
    total = sum(ref[...].astype(jnp.float32) for ref in refs[:count])
    refs[count][...] = (total * scale[...]).astype(jnp.bfloat16)


def scaled_sum(scale, parts):
    slots, emb, rows = parts[0].shape
    group = 7 if slots % 7 == 0 else slots
    block = pl.BlockSpec((group, emb, rows), lambda i: (i, 0, 0))
    return pl.pallas_call(
        functools.partial(scaled_body, len(parts)),
        grid=(slots // group,),
        in_specs=[whole((1, 1, rows))] + [block] * len(parts),
        out_specs=block,
        out_shape=jax.ShapeDtypeStruct((slots, emb, rows), jnp.bfloat16),
        compiler_params=pltpu.CompilerParams(vmem_limit_bytes=VMEM_LIMIT),
    )(scale.reshape(1, 1, rows), *parts)


def across(value, shift):
    count = lax.axis_size("table")
    return lax.ppermute(value, "table", [(i, (i + shift) % count) for i in range(count)])


def swap(bits, value, shift=0):
    copies, tables = lax.axis_size("copy"), lax.axis_size("table")
    pairs = [
        (c * tables + i, (c ^ bits) * tables + (i + shift) % tables)
        for c in range(copies)
        for i in range(tables)
    ]
    return lax.ppermute(value, ("copy", "table"), pairs)


def after(value, other):
    return lax.optimization_barrier((value, other))[0]


def by_distance(run, distance, *values):
    branches = [functools.partial(run, bits) for bits in range(1, lax.axis_size("copy"))]
    return lax.switch(distance - 1, branches, *values)


def swap_logits(bits, z_own, t_own):
    shifts = range(lax.axis_size("table"))
    t_parts = [swap(bits, t_own, k) for k in shifts]
    return [z_own] + [across(z_own, k) for k in shifts if k], t_parts


def on_device(pooled, slot_of_table, partner, labels, w_first, b_first, w_head):
    tables = lax.axis_size("table")
    rows, slots, emb = pooled.shape
    me_copy = lax.axis_index("copy")
    distance = jnp.bitwise_xor(me_copy, partner[me_copy])

    own = jnp.transpose(pooled, (1, 0, 2))
    blocks = [own] + [across(own, k) for k in range(1, tables)]
    cuts = [0, (5 * slots) // 7, slots] if slots % 7 == 0 else [0, slots]
    theirs = []
    for first, last in zip(cuts, cuts[1:]):
        piece = own[first:last]
        if theirs:
            piece = after(piece, theirs[-1])
        theirs.append(by_distance(swap, distance, piece))
    their_blocks = [theirs] + [[across(piece, k) for piece in theirs] for k in range(1, tables)]

    z_own, slope, active, feats, w, *parts = student(
        slot_of_table, blocks, w_first[0], b_first, w_head
    )
    parts = parts[:1] + [across(part, k) for k, part in enumerate(parts) if k]
    t_own = teacher(slot_of_table, their_blocks, w, b_first, w_head)
    z_parts, t_parts = by_distance(swap_logits, distance, z_own, t_own)

    low, grad_bias, grad_head, loss, scale = row_grads(
        z_parts, t_parts, labels.reshape(1, rows), slope, active
    )
    grad_first = lax.dot_general(
        feats, low, (((0,), (0,)), ((), ())), preferred_element_type=jnp.float32
    ).astype(jnp.bfloat16)
    pooled_grad = scaled_sum(scale, parts)
    return (pooled_grad, grad_first[None], grad_bias, grad_head, loss.reshape(1))


def solution(mesh):
    in_specs = (
        P("copy", "table", None),
        P(),
        P(),
        P("copy"),
        P("copy", None, "table"),
        P("copy", "table"),
        P("copy", "table"),
    )
    out_specs = (
        P("table", None, "copy"),
        P("copy", None, "table"),
        P("copy", "table"),
        P("copy", "table"),
        P("copy"),
    )
    return jax.shard_map(
        on_device, mesh=mesh, in_specs=in_specs, out_specs=out_specs, check_vma=False
    )
```

```python
import functools

import jax
import jax.numpy as jnp
from jax import lax
from jax.experimental import pallas as pl
from jax.experimental.pallas import tpu as pltpu
from jax.sharding import PartitionSpec as P

VMEM_LIMIT = 10 * 1024 * 1024
VMEM = pl.BlockSpec(memory_space=pltpu.VMEM)
SMEM = pl.BlockSpec(memory_space=pltpu.SMEM)
HBM = pl.BlockSpec(memory_space=pltpu.HBM)
TILE = 256


def in_hbm(value):
    return pltpu.with_memory_space_constraint(value, pltpu.HBM)


def whole(shape):
    return pl.BlockSpec(shape, lambda *_: (0,) * len(shape))


def tiles(width):
    return TILE if width % TILE == 0 else width


def part_of(i, size):
    return pl.ds(pl.multiple_of(i * size, size), size)


def copy_features(slot_of, blocks, feats):
    me, tables = lax.axis_index("table"), lax.axis_size("table")
    emb = blocks[0][0].shape[2]
    slots = sum(piece.shape[0] for piece in blocks[0])

    @pl.loop(0, feats.shape[1] // emb)
    def _(t):
        slot = slot_of[t]
        place = lax.rem(slot, slots)
        group = lax.rem(me + tables - slot // slots, tables)
        for k, pieces in enumerate(blocks):
            first = 0
            for piece in pieces:
                last = first + piece.shape[0]

                @pl.when((group == k) & (place >= first) & (place < last))
                def _():
                    feats[:, part_of(t, emb)] = piece[place - first]

                first = last


def forward_tiles(feats, w, b, held, finish, arrive=lambda i: None):
    tile = held.shape[1]
    count = w.shape[1] // tile

    def product(i):
        arrive(i)
        cut = part_of(i, tile)
        value = jnp.dot(feats[...], w[:, cut], preferred_element_type=jnp.float32)
        return value + b[:, cut].astype(jnp.float32)

    held[...] = product(0)

    @pl.loop(1, count)
    def _(i):
        before = held[...]
        value = product(i)
        finish(i - 1, before)
        held[...] = value

    finish(count - 1, held[...])


def swish(pre):
    sigmoid = 0.5 * jnp.tanh(0.5 * pre) + 0.5
    return sigmoid, pre * sigmoid


def add_lanes(total, wide):
    for lane in range(0, wide.shape[1], 128):
        total[...] += wide[:, lane : lane + 128]


def student_body(pieces, slot_of, *refs):
    given, refs = refs[: 3 + len(pieces)], refs[3 + len(pieces) :]
    logit, slope, active, feats, w, *refs = refs
    grads = [[refs.pop(0) for _ in sizes] for sizes in pieces]
    held, total, turned, blocks, b, h, here, arrived = refs
    emb = grads[0][0].shape[1]
    slots = blocks.shape[1]
    tile = held.shape[1]
    wanted = [b, h] + [blocks.at[k] for k in range(len(pieces))]
    small = [
        pltpu.make_async_copy(source, goal, here.at[i])
        for i, (source, goal) in enumerate(zip(given[1:], wanted))
    ]
    for copy in small:
        copy.start()

    def fetch(i):
        cut = part_of(i, tile)
        return pltpu.make_async_copy(given[0].at[:, cut], w.at[:, cut], arrived.at[i])

    @pl.loop(0, w.shape[1] // tile)
    def _(i):
        fetch(i).start()

    for copy in small:
        copy.wait()
    copy_features(slot_of, [[blocks.at[k]] for k in range(len(pieces))], feats)
    total[...] = jnp.zeros_like(total)

    def finish(i, pre):
        cut = part_of(i, pre.shape[1])
        head = h[:, cut].astype(jnp.float32)
        sigmoid, act = swish(pre)
        add_lanes(total, act * head)
        low = (head * (sigmoid + act * (1.0 - sigmoid))).astype(jnp.bfloat16)
        slope[:, cut] = low
        turned[cut, :] = low.T
        active[:, cut] = act.astype(jnp.bfloat16)

    forward_tiles(feats, w, b, held, finish, lambda i: fetch(i).wait())
    logit[...] = jnp.sum(total[...].T, axis=0, keepdims=True)

    for grad in sum(grads, []):
        grad[...] = jnp.zeros_like(grad)

    me, tables = lax.axis_index("table"), lax.axis_size("table")
    used = w.shape[0] // emb
    group = max(n for n in range(1, 14) if used % n == 0)

    @pl.loop(0, used // group)
    def _(i):
        value = jnp.dot(
            w[part_of(i, group * emb), :], turned[...], preferred_element_type=jnp.float32
        ).astype(jnp.bfloat16)
        for j in range(group):
            slot = slot_of[group * i + j]
            owner = lax.rem(slot // slots + tables - me, tables)
            place = lax.rem(slot, slots)
            for k in range(len(grads)):
                first = 0
                for grad in grads[k]:
                    last = first + grad.shape[0]

                    @pl.when((owner == k) & (place >= first) & (place < last))
                    def _():
                        grad[place - first] = value[j * emb : (j + 1) * emb, :]

                    first = last


def student(slot_of, blocks, w, b, h):
    slots, rows, emb = blocks[0].shape
    depth, units = w.shape
    halves = [slots // 2] * 2 if slots % 2 == 0 else [slots]
    pieces = [[slots]] + [halves] * (len(blocks) - 1)
    shape = jax.ShapeDtypeStruct
    given = [in_hbm(value) for value in (w, b, h, *blocks)]
    results = pl.pallas_call(
        functools.partial(student_body, pieces),
        in_specs=[SMEM] + [HBM] * len(given),
        out_specs=[VMEM] * (5 + sum(len(sizes) for sizes in pieces)),
        out_shape=[
            shape((1, rows), jnp.float32),
            shape((rows, units), jnp.bfloat16),
            shape((rows, units), jnp.bfloat16),
            shape((rows, depth), jnp.bfloat16),
            shape((depth, units), jnp.bfloat16),
        ]
        + [shape((size, emb, rows), jnp.bfloat16) for sizes in pieces for size in sizes],
        scratch_shapes=[
            pltpu.VMEM((rows, tiles(units)), jnp.float32),
            pltpu.VMEM((rows, 128), jnp.float32),
            pltpu.VMEM((units, rows), jnp.bfloat16),
            pltpu.VMEM((len(blocks), slots, rows, emb), jnp.bfloat16),
            pltpu.VMEM((1, units), jnp.bfloat16),
            pltpu.VMEM((1, units), jnp.bfloat16),
            pltpu.SemaphoreType.DMA((2 + len(blocks),)),
            pltpu.SemaphoreType.DMA((units // tiles(units),)),
        ],
        compiler_params=pltpu.CompilerParams(vmem_limit_bytes=VMEM_LIMIT),
        cost_estimate=pl.CostEstimate(
            flops=4 * rows * depth * units,
            bytes_accessed=2 * depth * units,
            transcendentals=rows * units,
        ),
    )(slot_of, *given)
    grads = list(results[5:])
    return *results[:5], [[grads.pop(0) for _ in sizes] for sizes in pieces]


def teacher_body(pieces, slot_of, *refs):
    count = sum(pieces)
    blocks, (w, b, h, logit, feats, held, total) = list(refs[:count]), refs[count:]
    copy_features(slot_of, [[blocks.pop(0) for _ in range(n)] for n in pieces], feats)
    total[...] = jnp.zeros_like(total)

    def finish(i, pre):
        head = h[:, part_of(i, pre.shape[1])].astype(jnp.float32)
        add_lanes(total, swish(pre)[1] * head)

    forward_tiles(feats, w, b, held, finish)
    logit[...] = jnp.sum(total[...].T, axis=0, keepdims=True)


def teacher(slot_of, blocks, w, b, h):
    rows = blocks[0][0].shape[1]
    depth, units = w.shape
    pieces = [len(block) for block in blocks]
    count = sum(pieces)
    return pl.pallas_call(
        functools.partial(teacher_body, pieces),
        in_specs=[SMEM] + [VMEM] * (count + 3),
        out_specs=VMEM,
        out_shape=jax.ShapeDtypeStruct((1, rows), jnp.float32),
        scratch_shapes=[
            pltpu.VMEM((rows, depth), jnp.bfloat16),
            pltpu.VMEM((rows, tiles(units)), jnp.float32),
            pltpu.VMEM((rows, 128), jnp.float32),
        ],
        compiler_params=pltpu.CompilerParams(vmem_limit_bytes=VMEM_LIMIT),
        cost_estimate=pl.CostEstimate(
            flops=2 * rows * depth * units,
            bytes_accessed=2 * depth * units,
            transcendentals=rows * units,
        ),
    )(slot_of, *(piece for block in blocks for piece in block), w, b, h)


def rows_body(count, y_ref, *refs):
    zs, ts, refs = refs[:count], refs[count : 2 * count], refs[2 * count :]
    slope, active, low, bias, head, loss, scale = refs
    rows = y_ref.shape[1]
    z = sum(ref[...] for ref in zs)
    soft = jax.nn.sigmoid(sum(ref[...] for ref in ts))
    y = y_ref[...].astype(jnp.float32)
    grads = 2.0 * jax.nn.sigmoid(z) - y - soft
    scale[...] = grads
    softplus = jnp.maximum(z, 0.0) + jnp.log1p(jnp.exp(-jnp.abs(z)))
    losses = 2.0 * softplus - y * z - soft * z
    loss[...] = jnp.sum(losses, axis=1, keepdims=True) / rows
    column = jnp.broadcast_to(grads, (128, rows)).T

    @pl.loop(0, slope.shape[1] // 128)
    def _(i):
        cut = part_of(i, 128)
        pre = slope[:, cut].astype(jnp.float32) * column
        low[:, cut] = pre.astype(jnp.bfloat16)
        bias[:, cut] = jnp.sum(pre, axis=0, keepdims=True)
        head[:, cut] = jnp.sum(
            active[:, cut].astype(jnp.float32) * column, axis=0, keepdims=True
        )


def row_grads(z_parts, t_parts, labels, slope, active):
    rows, units = slope.shape
    shape = jax.ShapeDtypeStruct
    row, units_row = whole((1, rows)), whole((1, units))
    return pl.pallas_call(
        functools.partial(rows_body, len(z_parts)),
        grid=(1,),
        in_specs=[row] * (1 + len(z_parts) + len(t_parts)) + [VMEM] * 2,
        out_specs=[VMEM, units_row, units_row, whole((1, 1)), row],
        out_shape=[
            shape((rows, units), jnp.bfloat16),
            shape((1, units), jnp.float32),
            shape((1, units), jnp.float32),
            shape((1, 1), jnp.float32),
            shape((1, rows), jnp.float32),
        ],
        compiler_params=pltpu.CompilerParams(vmem_limit_bytes=VMEM_LIMIT),
    )(labels, *z_parts, *t_parts, slope, active)


def scaled_body(size, scale, kept, *refs):
    others, out = refs[:-1], refs[-1]
    factor = scale[...]
    for i in range(kept.shape[0] // size):
        cut = slice(i * size, (i + 1) * size)
        total = kept[cut].astype(jnp.float32)
        for pieces in others[i :: kept.shape[0] // size]:
            total = total + pieces[...].astype(jnp.float32)
        out[cut] = (total * factor).astype(jnp.bfloat16)


def scaled_sum(scale, kept, others):
    slots, emb, rows = kept.shape
    size = others[0][0].shape[0]
    flat = [piece for pieces in others for piece in pieces]
    return pl.pallas_call(
        functools.partial(scaled_body, size),
        in_specs=[VMEM] * (2 + len(flat)),
        out_specs=VMEM,
        out_shape=jax.ShapeDtypeStruct((slots, emb, rows), jnp.bfloat16),
        compiler_params=pltpu.CompilerParams(vmem_limit_bytes=VMEM_LIMIT),
    )(scale.reshape(1, 1, rows), kept, *flat)


def across(value, shift):
    count = lax.axis_size("table")
    return lax.ppermute(value, "table", [(i, (i + shift) % count) for i in range(count)])


def swap(bits, value, shift=0):
    copies, tables = lax.axis_size("copy"), lax.axis_size("table")
    pairs = [
        (c * tables + i, (c ^ bits) * tables + (i + shift) % tables)
        for c in range(copies)
        for i in range(tables)
    ]
    return lax.ppermute(value, ("copy", "table"), pairs)


def after(value, other):
    return lax.optimization_barrier((value, other))[0]


def by_distance(run, distance, *values):
    branches = [functools.partial(run, bits) for bits in range(1, lax.axis_size("copy"))]
    return lax.switch(distance - 1, branches, *values)


def swap_rows(bits, own):
    cut = (4 * own.shape[0]) // 7
    first = swap(bits, own[:cut])
    other = across(own, 1)
    second = swap(bits, after(own[cut:], first))
    return other, first, second, across(first, 1)


def swap_logits(bits, z_own, t_own):
    return across(z_own, 1), swap(bits, t_own), swap(bits, t_own, 1)


def on_device(pooled, slot_of_table, partner, labels, w_first, b_first, w_head):
    tables = lax.axis_size("table")
    rows, slots, emb = pooled.shape
    me_copy = lax.axis_index("copy")
    distance = jnp.bitwise_xor(me_copy, partner[me_copy])

    own = jnp.transpose(pooled, (1, 0, 2))
    if tables == 2:
        other, first, second, first_other = by_distance(swap_rows, distance, own)
        blocks = [own, other]
        their_blocks = [[first, second], [first_other, across(second, 1)]]
    else:
        theirs = by_distance(swap, distance, own)
        blocks = [own] + [across(own, k) for k in range(1, tables)]
        their_blocks = [[theirs]] + [[across(theirs, k)] for k in range(1, tables)]

    z_own, slope, active, feats, w, grads = student(
        slot_of_table, blocks, w_first[0], b_first, w_head
    )
    early = [across(pieces[0], k) for k, pieces in enumerate(grads) if k]
    t_own = teacher(slot_of_table, their_blocks, w, b_first, w_head)
    if tables == 2:
        z_other, *t_parts = by_distance(swap_logits, distance, z_own, t_own)
        z_parts = [z_own, z_other]
    else:
        z_own, t_own = lax.psum((z_own, t_own), "table")
        z_parts, t_parts = [z_own], [by_distance(swap, distance, t_own)]
    others = [
        [piece] + [across(after(rest, t_parts[-1]), k) for rest in grads[k][1:]]
        for k, piece in enumerate(early, 1)
    ]

    low, grad_bias, grad_head, loss, scale = row_grads(
        z_parts, t_parts, labels.reshape(1, rows), slope, active
    )
    grad_first = lax.dot_general(
        feats, low, (((0,), (0,)), ((), ())), preferred_element_type=jnp.float32
    ).astype(jnp.bfloat16)
    pooled_grad = scaled_sum(scale, grads[0][0], others)
    return (pooled_grad, grad_first[None], grad_bias, grad_head, loss.reshape(1))


def solution(mesh):
    in_specs = (
        P("copy", "table", None),
        P(),
        P(),
        P("copy"),
        P("copy", None, "table"),
        P("copy", "table"),
        P("copy", "table"),
    )
    out_specs = (
        P("table", None, "copy"),
        P("copy", None, "table"),
        P("copy", "table"),
        P("copy", "table"),
        P("copy"),
    )
    return jax.shard_map(
        on_device, mesh=mesh, in_specs=in_specs, out_specs=out_specs, check_vma=False
    )
```

```python
import functools

import jax
import jax.numpy as jnp
from jax import lax
from jax.experimental import pallas as pl
from jax.experimental.pallas import tpu as pltpu
from jax.sharding import PartitionSpec as P

VMEM_LIMIT = 10 * 1024 * 1024
VMEM = pl.BlockSpec(memory_space=pltpu.VMEM)
SMEM = pl.BlockSpec(memory_space=pltpu.SMEM)
HBM = pl.BlockSpec(memory_space=pltpu.HBM)
TILE = 256


def in_hbm(value):
    return pltpu.with_memory_space_constraint(value, pltpu.HBM)


def whole(shape):
    return pl.BlockSpec(shape, lambda *_: (0,) * len(shape))


def tiles(width):
    return TILE if width % TILE == 0 else width


def part_of(i, size):
    return pl.ds(pl.multiple_of(i * size, size), size)


def copy_features(slot_of, blocks, feats):
    me, tables = lax.axis_index("table"), lax.axis_size("table")
    emb = blocks[0][0].shape[2]
    slots = sum(piece.shape[0] for piece in blocks[0])

    @pl.loop(0, feats.shape[1] // emb)
    def _(t):
        slot = slot_of[t]
        place = lax.rem(slot, slots)
        group = lax.rem(me + tables - slot // slots, tables)
        for k, pieces in enumerate(blocks):
            first = 0
            for piece in pieces:
                last = first + piece.shape[0]

                @pl.when((group == k) & (place >= first) & (place < last))
                def _():
                    feats[:, part_of(t, emb)] = piece[place - first]

                first = last


def forward_tiles(feats, w, b, held, finish, arrive=lambda i: None):
    tile = held.shape[1]
    count = w.shape[1] // tile

    def product(i):
        arrive(i)
        cut = part_of(i, tile)
        value = jnp.dot(feats[...], w[:, cut], preferred_element_type=jnp.float32)
        return value + b[:, cut].astype(jnp.float32)

    held[...] = product(0)

    @pl.loop(1, count)
    def _(i):
        before = held[...]
        value = product(i)
        finish(i - 1, before)
        held[...] = value

    finish(count - 1, held[...])


def swish(pre):
    sigmoid = 0.5 * jnp.tanh(0.5 * pre) + 0.5
    return sigmoid, pre * sigmoid


def add_lanes(total, wide):
    for lane in range(0, wide.shape[1], 128):
        total[...] += wide[:, lane : lane + 128]


def student_body(pieces, slot_of, *refs):
    given, refs = refs[: 3 + len(pieces)], refs[3 + len(pieces) :]
    logit, slope, active_out, feats, w, *refs = refs
    grads = [[refs.pop(0) for _ in sizes] for sizes in pieces]
    held, total, turned, active, blocks, b, h, here, arrived = refs
    emb = grads[0][0].shape[1]
    slots = blocks.shape[1]
    tile = held.shape[1]
    wanted = [b, h] + [blocks.at[k] for k in range(len(pieces))]
    small = [
        pltpu.make_async_copy(source, goal, here.at[i])
        for i, (source, goal) in enumerate(zip(given[1:], wanted))
    ]
    for copy in small:
        copy.start()

    def fetch(i):
        cut = part_of(i, tile)
        return pltpu.make_async_copy(given[0].at[:, cut], w.at[:, cut], arrived.at[i])

    @pl.loop(0, w.shape[1] // tile)
    def _(i):
        fetch(i).start()

    for copy in small:
        copy.wait()
    copy_features(slot_of, [[blocks.at[k]] for k in range(len(pieces))], feats)
    total[...] = jnp.zeros_like(total)

    def finish(i, pre):
        cut = part_of(i, pre.shape[1])
        head = h[:, cut].astype(jnp.float32)
        sigmoid, act = swish(pre)
        add_lanes(total, act * head)
        low = (head * (sigmoid + act * (1.0 - sigmoid))).astype(jnp.bfloat16)
        slope[:, cut] = low
        turned[cut, :] = low.T
        active[:, cut] = act.astype(jnp.bfloat16)

    forward_tiles(feats, w, b, held, finish, lambda i: fetch(i).wait())
    logit[...] = jnp.sum(total[...].T, axis=0, keepdims=True)

    keep = pltpu.make_async_copy(active, active_out, here.at[len(small)])
    keep.start()
    for grad in sum(grads, []):
        grad[...] = jnp.zeros_like(grad)

    me, tables = lax.axis_index("table"), lax.axis_size("table")
    used = w.shape[0] // emb
    group = max(n for n in range(1, 14) if used % n == 0)

    @pl.loop(0, used // group)
    def _(i):
        value = jnp.dot(
            w[part_of(i, group * emb), :], turned[...], preferred_element_type=jnp.float32
        ).astype(jnp.bfloat16)
        for j in range(group):
            slot = slot_of[group * i + j]
            owner = lax.rem(slot // slots + tables - me, tables)
            place = lax.rem(slot, slots)
            for k in range(len(grads)):
                first = 0
                for grad in grads[k]:
                    last = first + grad.shape[0]

                    @pl.when((owner == k) & (place >= first) & (place < last))
                    def _():
                        grad[place - first] = value[j * emb : (j + 1) * emb, :]

                    first = last

    keep.wait()


def student(slot_of, blocks, w, b, h):
    slots, rows, emb = blocks[0].shape
    depth, units = w.shape
    first = (3 * slots) // 7
    sizes = [first, slots - first] if len(blocks) == 2 else [slots]
    pieces = [[slots]] + [sizes] * (len(blocks) - 1)
    shape = jax.ShapeDtypeStruct
    given = [in_hbm(value) for value in (w, b, h, blocks[0])] + blocks[1:]
    results = pl.pallas_call(
        functools.partial(student_body, pieces),
        in_specs=[SMEM] + [HBM] * 4 + [pl.BlockSpec(memory_space=pl.ANY)] * (len(given) - 4),
        out_specs=[VMEM, VMEM, HBM] + [VMEM] * (2 + sum(len(sizes) for sizes in pieces)),
        out_shape=[
            shape((1, rows), jnp.float32),
            shape((rows, units), jnp.bfloat16),
            pltpu.HBM((rows, units), jnp.bfloat16),
            shape((rows, depth), jnp.bfloat16),
            shape((depth, units), jnp.bfloat16),
        ]
        + [shape((size, emb, rows), jnp.bfloat16) for sizes in pieces for size in sizes],
        scratch_shapes=[
            pltpu.VMEM((rows, tiles(units)), jnp.float32),
            pltpu.VMEM((rows, 128), jnp.float32),
            pltpu.VMEM((units, rows), jnp.bfloat16),
            pltpu.VMEM((rows, units), jnp.bfloat16),
            pltpu.VMEM((len(blocks), slots, rows, emb), jnp.bfloat16),
            pltpu.VMEM((1, units), jnp.bfloat16),
            pltpu.VMEM((1, units), jnp.bfloat16),
            pltpu.SemaphoreType.DMA((3 + len(blocks),)),
            pltpu.SemaphoreType.DMA((units // tiles(units),)),
        ],
        compiler_params=pltpu.CompilerParams(vmem_limit_bytes=VMEM_LIMIT),
        cost_estimate=pl.CostEstimate(
            flops=4 * rows * depth * units,
            bytes_accessed=2 * depth * units,
            transcendentals=rows * units,
        ),
    )(slot_of, *given)
    grads = list(results[5:])
    return *results[:5], [[grads.pop(0) for _ in sizes] for sizes in pieces]


def teacher_body(pieces, slot_of, *refs):
    count = sum(pieces)
    blocks, (w, b, h, logit, feats, held, total) = list(refs[:count]), refs[count:]
    copy_features(slot_of, [[blocks.pop(0) for _ in range(n)] for n in pieces], feats)
    total[...] = jnp.zeros_like(total)

    def finish(i, pre):
        head = h[:, part_of(i, pre.shape[1])].astype(jnp.float32)
        add_lanes(total, swish(pre)[1] * head)

    forward_tiles(feats, w, b, held, finish)
    logit[...] = jnp.sum(total[...].T, axis=0, keepdims=True)


def teacher(slot_of, blocks, w, b, h):
    rows = blocks[0][0].shape[1]
    depth, units = w.shape
    pieces = [len(block) for block in blocks]
    count = sum(pieces)
    return pl.pallas_call(
        functools.partial(teacher_body, pieces),
        in_specs=[SMEM] + [VMEM] * (count + 3),
        out_specs=VMEM,
        out_shape=jax.ShapeDtypeStruct((1, rows), jnp.float32),
        scratch_shapes=[
            pltpu.VMEM((rows, depth), jnp.bfloat16),
            pltpu.VMEM((rows, tiles(units)), jnp.float32),
            pltpu.VMEM((rows, 128), jnp.float32),
        ],
        compiler_params=pltpu.CompilerParams(vmem_limit_bytes=VMEM_LIMIT),
        cost_estimate=pl.CostEstimate(
            flops=2 * rows * depth * units,
            bytes_accessed=2 * depth * units,
            transcendentals=rows * units,
        ),
    )(slot_of, *(piece for block in blocks for piece in block), w, b, h)


def rows_body(count, y_ref, *refs):
    zs, ts, refs = refs[:count], refs[count : 2 * count], refs[2 * count :]
    slope, active_in, low, bias, head, loss, scale, active, here = refs
    rows = y_ref.shape[1]
    fetch = pltpu.make_async_copy(active_in, active, here)
    fetch.start()
    z = sum(ref[...] for ref in zs)
    soft = jax.nn.sigmoid(sum(ref[...] for ref in ts))
    y = y_ref[...].astype(jnp.float32)
    grads = 2.0 * jax.nn.sigmoid(z) - y - soft
    scale[...] = grads
    softplus = jnp.maximum(z, 0.0) + jnp.log1p(jnp.exp(-jnp.abs(z)))
    losses = 2.0 * softplus - y * z - soft * z
    loss[...] = jnp.sum(losses, axis=1, keepdims=True) / rows
    column = jnp.broadcast_to(grads, (128, rows)).T

    @pl.loop(0, slope.shape[1] // 128)
    def _(i):
        cut = part_of(i, 128)
        pre = slope[:, cut].astype(jnp.float32) * column
        low[:, cut] = pre.astype(jnp.bfloat16)
        bias[:, cut] = jnp.sum(pre, axis=0, keepdims=True)

    fetch.wait()

    @pl.loop(0, slope.shape[1] // 128)
    def _(i):
        cut = part_of(i, 128)
        head[:, cut] = jnp.sum(
            active[:, cut].astype(jnp.float32) * column, axis=0, keepdims=True
        )


def row_grads(z_parts, t_parts, labels, slope, active):
    rows, units = slope.shape
    shape = jax.ShapeDtypeStruct
    row, units_row = whole((1, rows)), whole((1, units))
    return pl.pallas_call(
        functools.partial(rows_body, len(z_parts)),
        grid=(1,),
        in_specs=[row] * (1 + len(z_parts) + len(t_parts)) + [VMEM, HBM],
        out_specs=[VMEM, units_row, units_row, whole((1, 1)), row],
        out_shape=[
            shape((rows, units), jnp.bfloat16),
            shape((1, units), jnp.float32),
            shape((1, units), jnp.float32),
            shape((1, 1), jnp.float32),
            shape((1, rows), jnp.float32),
        ],
        scratch_shapes=[pltpu.VMEM((rows, units), jnp.bfloat16), pltpu.SemaphoreType.DMA],
        compiler_params=pltpu.CompilerParams(vmem_limit_bytes=VMEM_LIMIT),
    )(labels, *z_parts, *t_parts, slope, in_hbm(active))


def scaled_body(sizes, scale, kept, *refs):
    others, out = refs[:-1], refs[-1]
    factor, first = scale[...], 0
    for i, size in enumerate(sizes):
        cut = slice(first, first + size)
        total = kept[cut].astype(jnp.float32)
        for piece in others[i :: len(sizes)]:
            total = total + piece[...].astype(jnp.float32)
        out[cut] = (total * factor).astype(jnp.bfloat16)
        first += size


def scaled_sum(scale, kept, others):
    slots, emb, rows = kept.shape
    flat = [piece for pieces in others for piece in pieces]
    return pl.pallas_call(
        functools.partial(scaled_body, [piece.shape[0] for piece in others[0]]),
        in_specs=[VMEM] * (2 + len(flat)),
        out_specs=VMEM,
        out_shape=jax.ShapeDtypeStruct((slots, emb, rows), jnp.bfloat16),
        compiler_params=pltpu.CompilerParams(vmem_limit_bytes=VMEM_LIMIT),
    )(scale.reshape(1, 1, rows), kept, *flat)


def across(value, shift):
    count = lax.axis_size("table")
    return lax.ppermute(value, "table", [(i, (i + shift) % count) for i in range(count)])


def swap(bits, value, shift=0):
    copies, tables = lax.axis_size("copy"), lax.axis_size("table")
    pairs = [
        (c * tables + i, (c ^ bits) * tables + (i + shift) % tables)
        for c in range(copies)
        for i in range(tables)
    ]
    return lax.ppermute(value, ("copy", "table"), pairs)


def after(value, other):
    return lax.optimization_barrier((value, other))[0]


def by_distance(run, distance, *values):
    branches = [functools.partial(run, bits) for bits in range(1, lax.axis_size("copy"))]
    return lax.switch(distance - 1, branches, *values)


def swap_logits(bits, z_own, t_own):
    return across(z_own, 1), swap(bits, t_own), swap(bits, t_own, 1)


def on_device(pooled, slot_of_table, partner, labels, w_first, b_first, w_head):
    tables = lax.axis_size("table")
    rows, slots, emb = pooled.shape
    me_copy = lax.axis_index("copy")
    distance = jnp.bitwise_xor(me_copy, partner[me_copy])

    own = jnp.transpose(pooled, (1, 0, 2))
    blocks = [own] + [across(own, k) for k in range(1, tables)]
    cuts = [0, (4 * slots) // 7, slots] if tables == 2 else [0, slots]
    theirs = []
    for first, last in zip(cuts, cuts[1:]):
        piece = own[first:last]
        if theirs:
            piece = after(piece, theirs[-1])
        theirs.append(by_distance(swap, distance, piece))
    their_blocks = [theirs] + [[across(piece, k) for piece in theirs] for k in range(1, tables)]

    z_own, slope, active, feats, w, grads = student(
        slot_of_table, blocks, w_first[0], b_first, w_head
    )
    early = [across(pieces[0], k) for k, pieces in enumerate(grads) if k]
    t_own = teacher(slot_of_table, their_blocks, w, b_first, w_head)
    for piece in early:
        t_own = after(t_own, piece)
    if tables == 2:
        z_other, *t_parts = by_distance(swap_logits, distance, z_own, t_own)
        z_parts = [z_own, z_other]
    else:
        z_own, t_own = lax.psum((z_own, t_own), "table")
        z_parts, t_parts = [z_own], [by_distance(swap, distance, t_own)]
    others = [
        [piece] + [across(after(rest, t_parts[-1]), k) for rest in grads[k][1:]]
        for k, piece in enumerate(early, 1)
    ]

    low, grad_bias, grad_head, loss, scale = row_grads(
        z_parts, t_parts, labels.reshape(1, rows), slope, active
    )
    grad_first = lax.dot_general(
        feats, low, (((0,), (0,)), ((), ())), preferred_element_type=jnp.float32
    ).astype(jnp.bfloat16)
    pooled_grad = scaled_sum(scale, grads[0][0], others)
    return (pooled_grad, grad_first[None], grad_bias, grad_head, loss.reshape(1))


def solution(mesh):
    in_specs = (
        P("copy", "table", None),
        P(),
        P(),
        P("copy"),
        P("copy", None, "table"),
        P("copy", "table"),
        P("copy", "table"),
    )
    out_specs = (
        P("table", None, "copy"),
        P("copy", None, "table"),
        P("copy", "table"),
        P("copy", "table"),
        P("copy"),
    )
    return jax.shard_map(
        on_device, mesh=mesh, in_specs=in_specs, out_specs=out_specs, check_vma=False
    )
```

```python
import functools

import jax
import jax.numpy as jnp
from jax import lax
from jax.experimental import pallas as pl
from jax.experimental.pallas import tpu as pltpu
from jax.sharding import PartitionSpec as P

VMEM_LIMIT = 10 * 1024 * 1024
VMEM = pl.BlockSpec(memory_space=pltpu.VMEM)
SMEM = pl.BlockSpec(memory_space=pltpu.SMEM)
HBM = pl.BlockSpec(memory_space=pltpu.HBM)
TILE = 256


def in_hbm(value):
    return pltpu.with_memory_space_constraint(value, pltpu.HBM)


def whole(shape):
    return pl.BlockSpec(shape, lambda *_: (0,) * len(shape))


def tiles(width):
    return TILE if width % TILE == 0 else width


def part_of(i, size):
    return pl.ds(pl.multiple_of(i * size, size), size)


def copy_features(slot_of, blocks, feats):
    me, tables = lax.axis_index("table"), lax.axis_size("table")
    emb = blocks[0][0].shape[2]
    slots = sum(piece.shape[0] for piece in blocks[0])

    @pl.loop(0, feats.shape[1] // emb)
    def _(t):
        slot = slot_of[t]
        place = lax.rem(slot, slots)
        group = lax.rem(me + tables - slot // slots, tables)
        for k, pieces in enumerate(blocks):
            first = 0
            for piece in pieces:
                last = first + piece.shape[0]

                @pl.when((group == k) & (place >= first) & (place < last))
                def _():
                    feats[:, part_of(t, emb)] = piece[place - first]

                first = last


def forward_tiles(feats, w, b, held, finish, arrive=lambda i: None):
    tile = held.shape[1]
    count = w.shape[1] // tile

    def product(i):
        arrive(i)
        cut = part_of(i, tile)
        value = jnp.dot(feats[...], w[:, cut], preferred_element_type=jnp.float32)
        return value + b[:, cut].astype(jnp.float32)

    held[...] = product(0)

    @pl.loop(1, count)
    def _(i):
        before = held[...]
        value = product(i)
        finish(i - 1, before)
        held[...] = value

    finish(count - 1, held[...])


def swish(pre):
    sigmoid = 0.5 * jnp.tanh(0.5 * pre) + 0.5
    return sigmoid, pre * sigmoid


def add_lanes(total, wide):
    for lane in range(0, wide.shape[1], 128):
        total[...] += wide[:, lane : lane + 128]


def student_body(pieces, slot_of, *refs):
    given, refs = refs[: 3 + len(pieces)], refs[3 + len(pieces) :]
    logit, slope, active_out, feats, w, *refs = refs
    grads = [[refs.pop(0) for _ in sizes] for sizes in pieces]
    held, total, turned, active, blocks, b, h, here, arrived = refs
    emb = grads[0][0].shape[1]
    slots = blocks.shape[1]
    tile = held.shape[1]
    wanted = [b, h] + [blocks.at[k] for k in range(len(pieces))]
    small = [
        pltpu.make_async_copy(source, goal, here.at[i])
        for i, (source, goal) in enumerate(zip(given[1:], wanted))
    ]
    for copy in small:
        copy.start()

    def fetch(i):
        cut = part_of(i, tile)
        return pltpu.make_async_copy(given[0].at[:, cut], w.at[:, cut], arrived.at[i])

    @pl.loop(0, w.shape[1] // tile)
    def _(i):
        fetch(i).start()

    for copy in small:
        copy.wait()
    copy_features(slot_of, [[blocks.at[k]] for k in range(len(pieces))], feats)
    total[...] = jnp.zeros_like(total)

    def finish(i, pre):
        cut = part_of(i, pre.shape[1])
        head = h[:, cut].astype(jnp.float32)
        sigmoid, act = swish(pre)
        add_lanes(total, act * head)
        low = (head * (sigmoid + act * (1.0 - sigmoid))).astype(jnp.bfloat16)
        slope[:, cut] = low
        turned[cut, :] = low.T
        active[:, cut] = act.astype(jnp.bfloat16)

    forward_tiles(feats, w, b, held, finish, lambda i: fetch(i).wait())
    logit[...] = jnp.sum(total[...].T, axis=0, keepdims=True)

    keep = pltpu.make_async_copy(active, active_out, here.at[len(small)])
    keep.start()
    for grad in sum(grads, []):
        grad[...] = jnp.zeros_like(grad)

    me, tables = lax.axis_index("table"), lax.axis_size("table")
    used = w.shape[0] // emb
    group = max(n for n in range(1, 14) if used % n == 0)

    @pl.loop(0, used // group)
    def _(i):
        value = jnp.dot(
            w[part_of(i, group * emb), :], turned[...], preferred_element_type=jnp.float32
        ).astype(jnp.bfloat16)
        for j in range(group):
            slot = slot_of[group * i + j]
            owner = lax.rem(slot // slots + tables - me, tables)
            place = lax.rem(slot, slots)
            for k in range(len(grads)):
                first = 0
                for grad in grads[k]:
                    last = first + grad.shape[0]

                    @pl.when((owner == k) & (place >= first) & (place < last))
                    def _():
                        grad[place - first] = value[j * emb : (j + 1) * emb, :]

                    first = last

    keep.wait()


def student(slot_of, blocks, w, b, h):
    slots, rows, emb = blocks[0].shape
    depth, units = w.shape
    first = (3 * slots) // 7
    sizes = [first, slots - first] if len(blocks) == 2 else [slots]
    pieces = [[slots]] + [sizes] * (len(blocks) - 1)
    shape = jax.ShapeDtypeStruct
    given = [in_hbm(value) for value in (w, b, h, blocks[0])] + blocks[1:]
    results = pl.pallas_call(
        functools.partial(student_body, pieces),
        in_specs=[SMEM] + [HBM] * 4 + [pl.BlockSpec(memory_space=pl.ANY)] * (len(given) - 4),
        out_specs=[VMEM, VMEM, HBM] + [VMEM] * (2 + sum(len(sizes) for sizes in pieces)),
        out_shape=[
            shape((1, rows), jnp.float32),
            shape((rows, units), jnp.bfloat16),
            pltpu.HBM((rows, units), jnp.bfloat16),
            shape((rows, depth), jnp.bfloat16),
            shape((depth, units), jnp.bfloat16),
        ]
        + [shape((size, emb, rows), jnp.bfloat16) for sizes in pieces for size in sizes],
        scratch_shapes=[
            pltpu.VMEM((rows, tiles(units)), jnp.float32),
            pltpu.VMEM((rows, 128), jnp.float32),
            pltpu.VMEM((units, rows), jnp.bfloat16),
            pltpu.VMEM((rows, units), jnp.bfloat16),
            pltpu.VMEM((len(blocks), slots, rows, emb), jnp.bfloat16),
            pltpu.VMEM((1, units), jnp.bfloat16),
            pltpu.VMEM((1, units), jnp.bfloat16),
            pltpu.SemaphoreType.DMA((3 + len(blocks),)),
            pltpu.SemaphoreType.DMA((units // tiles(units),)),
        ],
        compiler_params=pltpu.CompilerParams(vmem_limit_bytes=VMEM_LIMIT),
        cost_estimate=pl.CostEstimate(
            flops=4 * rows * depth * units,
            bytes_accessed=2 * depth * units,
            transcendentals=rows * units,
        ),
    )(slot_of, *given)
    grads = list(results[5:])
    return *results[:5], [[grads.pop(0) for _ in sizes] for sizes in pieces]


def teacher_body(pieces, slot_of, *refs):
    count = sum(pieces)
    blocks, (w, b, h, logit, feats, held, total) = list(refs[:count]), refs[count:]
    copy_features(slot_of, [[blocks.pop(0) for _ in range(n)] for n in pieces], feats)
    total[...] = jnp.zeros_like(total)

    def finish(i, pre):
        head = h[:, part_of(i, pre.shape[1])].astype(jnp.float32)
        add_lanes(total, swish(pre)[1] * head)

    forward_tiles(feats, w, b, held, finish)
    logit[...] = jnp.sum(total[...].T, axis=0, keepdims=True)


def teacher(slot_of, blocks, w, b, h):
    rows = blocks[0][0].shape[1]
    depth, units = w.shape
    pieces = [len(block) for block in blocks]
    count = sum(pieces)
    return pl.pallas_call(
        functools.partial(teacher_body, pieces),
        in_specs=[SMEM] + [VMEM] * (count + 3),
        out_specs=VMEM,
        out_shape=jax.ShapeDtypeStruct((1, rows), jnp.float32),
        scratch_shapes=[
            pltpu.VMEM((rows, depth), jnp.bfloat16),
            pltpu.VMEM((rows, tiles(units)), jnp.float32),
            pltpu.VMEM((rows, 128), jnp.float32),
        ],
        compiler_params=pltpu.CompilerParams(vmem_limit_bytes=VMEM_LIMIT),
        cost_estimate=pl.CostEstimate(
            flops=2 * rows * depth * units,
            bytes_accessed=2 * depth * units,
            transcendentals=rows * units,
        ),
    )(slot_of, *(piece for block in blocks for piece in block), w, b, h)


def rows_body(count, y_ref, *refs):
    zs, ts, refs = refs[:count], refs[count : 2 * count], refs[2 * count :]
    slope, active_in, low, bias, head, loss, scale, active, here = refs
    rows = y_ref.shape[1]
    fetch = pltpu.make_async_copy(active_in, active, here)
    fetch.start()
    z = sum(ref[...] for ref in zs)
    soft = jax.nn.sigmoid(sum(ref[...] for ref in ts))
    y = y_ref[...].astype(jnp.float32)
    grads = 2.0 * jax.nn.sigmoid(z) - y - soft
    scale[...] = grads
    softplus = jnp.maximum(z, 0.0) + jnp.log1p(jnp.exp(-jnp.abs(z)))
    losses = 2.0 * softplus - y * z - soft * z
    loss[...] = jnp.sum(losses, axis=1, keepdims=True) / rows
    column = jnp.broadcast_to(grads, (128, rows)).T

    @pl.loop(0, slope.shape[1] // 128)
    def _(i):
        cut = part_of(i, 128)
        pre = slope[:, cut].astype(jnp.float32) * column
        low[:, cut] = pre.astype(jnp.bfloat16)
        bias[:, cut] = jnp.sum(pre, axis=0, keepdims=True)

    fetch.wait()

    @pl.loop(0, slope.shape[1] // 128)
    def _(i):
        cut = part_of(i, 128)
        head[:, cut] = jnp.sum(
            active[:, cut].astype(jnp.float32) * column, axis=0, keepdims=True
        )


def row_grads(z_parts, t_parts, labels, slope, active):
    rows, units = slope.shape
    shape = jax.ShapeDtypeStruct
    row, units_row = whole((1, rows)), whole((1, units))
    return pl.pallas_call(
        functools.partial(rows_body, len(z_parts)),
        grid=(1,),
        in_specs=[row] * (1 + len(z_parts) + len(t_parts)) + [VMEM, HBM],
        out_specs=[VMEM, units_row, units_row, whole((1, 1)), row],
        out_shape=[
            shape((rows, units), jnp.bfloat16),
            shape((1, units), jnp.float32),
            shape((1, units), jnp.float32),
            shape((1, 1), jnp.float32),
            shape((1, rows), jnp.float32),
        ],
        scratch_shapes=[pltpu.VMEM((rows, units), jnp.bfloat16), pltpu.SemaphoreType.DMA],
        compiler_params=pltpu.CompilerParams(vmem_limit_bytes=VMEM_LIMIT),
    )(labels, *z_parts, *t_parts, slope, in_hbm(active))


def scaled_body(sizes, scale, kept, *refs):
    others, out = refs[:-1], refs[-1]
    factor, first = scale[...], 0
    for i, size in enumerate(sizes):
        cut = slice(first, first + size)
        total = kept[cut].astype(jnp.float32)
        for piece in others[i :: len(sizes)]:
            total = total + piece[...].astype(jnp.float32)
        out[cut] = (total * factor).astype(jnp.bfloat16)
        first += size


def scaled_sum(scale, kept, others):
    slots, emb, rows = kept.shape
    flat = [piece for pieces in others for piece in pieces]
    return pl.pallas_call(
        functools.partial(scaled_body, [piece.shape[0] for piece in others[0]]),
        in_specs=[VMEM] * (2 + len(flat)),
        out_specs=VMEM,
        out_shape=jax.ShapeDtypeStruct((slots, emb, rows), jnp.bfloat16),
        compiler_params=pltpu.CompilerParams(vmem_limit_bytes=VMEM_LIMIT),
    )(scale.reshape(1, 1, rows), kept, *flat)


def across(value, shift):
    count = lax.axis_size("table")
    return lax.ppermute(value, "table", [(i, (i + shift) % count) for i in range(count)])


def swap(bits, value, shift=0):
    copies, tables = lax.axis_size("copy"), lax.axis_size("table")
    pairs = [
        (c * tables + i, (c ^ bits) * tables + (i + shift) % tables)
        for c in range(copies)
        for i in range(tables)
    ]
    return lax.ppermute(value, ("copy", "table"), pairs)


def after(value, other):
    return lax.optimization_barrier((value, other))[0]


def by_distance(run, distance, *values):
    branches = [functools.partial(run, bits) for bits in range(1, lax.axis_size("copy"))]
    return lax.switch(distance - 1, branches, *values)


def swap_rows(bits, own, piece):
    return across(own, 1), swap(bits, piece)


def swap_logits(bits, z_own, t_own):
    return across(z_own, 1), swap(bits, t_own), swap(bits, t_own, 1)


def on_device(pooled, slot_of_table, partner, labels, w_first, b_first, w_head):
    tables = lax.axis_size("table")
    rows, slots, emb = pooled.shape
    me_copy = lax.axis_index("copy")
    distance = jnp.bitwise_xor(me_copy, partner[me_copy])

    own = jnp.transpose(pooled, (1, 0, 2))
    if tables == 2:
        cut = (11 * slots) // 14
        other, first = by_distance(swap_rows, distance, own, own[:cut])
        second = by_distance(swap, distance, after(own[cut:], first))
        blocks = [own, other]
        theirs = [first, second]
    else:
        blocks = [own] + [across(own, k) for k in range(1, tables)]
        theirs = [by_distance(swap, distance, own)]
    their_blocks = [theirs] + [[across(piece, k) for piece in theirs] for k in range(1, tables)]

    z_own, slope, active, feats, w, grads = student(
        slot_of_table, blocks, w_first[0], b_first, w_head
    )
    early = [across(pieces[0], k) for k, pieces in enumerate(grads) if k]
    t_own = teacher(slot_of_table, their_blocks, w, b_first, w_head)
    for piece in early:
        t_own = after(t_own, piece)
    if tables == 2:
        z_other, *t_parts = by_distance(swap_logits, distance, z_own, t_own)
        z_parts = [z_own, z_other]
    else:
        z_own, t_own = lax.psum((z_own, t_own), "table")
        z_parts, t_parts = [z_own], [by_distance(swap, distance, t_own)]
    others = [
        [piece] + [across(after(rest, t_parts[-1]), k) for rest in grads[k][1:]]
        for k, piece in enumerate(early, 1)
    ]

    low, grad_bias, grad_head, loss, scale = row_grads(
        z_parts, t_parts, labels.reshape(1, rows), slope, active
    )
    grad_first = lax.dot_general(
        feats, low, (((0,), (0,)), ((), ())), preferred_element_type=jnp.float32
    ).astype(jnp.bfloat16)
    pooled_grad = scaled_sum(scale, grads[0][0], others)
    return (pooled_grad, grad_first[None], grad_bias, grad_head, loss.reshape(1))


def solution(mesh):
    in_specs = (
        P("copy", "table", None),
        P(),
        P(),
        P("copy"),
        P("copy", None, "table"),
        P("copy", "table"),
        P("copy", "table"),
    )
    out_specs = (
        P("table", None, "copy"),
        P("copy", None, "table"),
        P("copy", "table"),
        P("copy", "table"),
        P("copy"),
    )
    return jax.shard_map(
        on_device, mesh=mesh, in_specs=in_specs, out_specs=out_specs, check_vma=False
    )
```

```python
import functools

import jax
import jax.numpy as jnp
from jax import lax
from jax.experimental import pallas as pl
from jax.experimental.pallas import tpu as pltpu
from jax.sharding import PartitionSpec as P

VMEM_LIMIT = 10 * 1024 * 1024
VMEM = pl.BlockSpec(memory_space=pltpu.VMEM)
SMEM = pl.BlockSpec(memory_space=pltpu.SMEM)
HBM = pl.BlockSpec(memory_space=pltpu.HBM)
TILE = 256


def in_hbm(value):
    return pltpu.with_memory_space_constraint(value, pltpu.HBM)


def whole(shape):
    return pl.BlockSpec(shape, lambda *_: (0,) * len(shape))


def tiles(width):
    return TILE if width % TILE == 0 else width


def part_of(i, size):
    return pl.ds(pl.multiple_of(i * size, size), size)


def copy_features(slot_of, blocks, feats):
    me, tables = lax.axis_index("table"), lax.axis_size("table")
    emb = blocks[0][0].shape[2]
    slots = sum(piece.shape[0] for piece in blocks[0])

    @pl.loop(0, feats.shape[1] // emb)
    def _(t):
        slot = slot_of[t]
        place = lax.rem(slot, slots)
        group = lax.rem(me + tables - slot // slots, tables)
        for k, pieces in enumerate(blocks):
            first = 0
            for piece in pieces:
                last = first + piece.shape[0]

                @pl.when((group == k) & (place >= first) & (place < last))
                def _():
                    feats[:, part_of(t, emb)] = piece[place - first]

                first = last


def forward_tiles(feats, w, b, held, finish, arrive=lambda i: None):
    tile = held.shape[1]
    count = w.shape[1] // tile

    def product(i):
        arrive(i)
        cut = part_of(i, tile)
        value = jnp.dot(feats[...], w[:, cut], preferred_element_type=jnp.float32)
        return value + b[:, cut].astype(jnp.float32)

    held[...] = product(0)

    @pl.loop(1, count)
    def _(i):
        before = held[...]
        value = product(i)
        finish(i - 1, before)
        held[...] = value

    finish(count - 1, held[...])


def swish(pre):
    sigmoid = 0.5 * jnp.tanh(0.5 * pre) + 0.5
    return sigmoid, pre * sigmoid


def add_lanes(total, wide):
    for lane in range(0, wide.shape[1], 128):
        total[...] += wide[:, lane : lane + 128]


def in_terms(row):
    high = row.astype(jnp.bfloat16).astype(jnp.float32)
    middle = (row - high).astype(jnp.bfloat16).astype(jnp.float32)
    at = lax.broadcasted_iota(jnp.int32, (16, row.shape[1]), 0)
    terms = jnp.where(at == 0, high, jnp.where(at == 1, middle, row - high - middle))
    return terms.astype(jnp.bfloat16)


def from_terms(terms):
    wide = terms.astype(jnp.float32)
    return wide[0:1] + wide[1:2] + wide[2:3]


def student_body(pieces, slot_of, *refs):
    given, refs = refs[: 3 + len(pieces)], refs[3 + len(pieces) :]
    logit, slope, active_out, feats, w, *refs = refs
    grads = [[refs.pop(0) for _ in sizes] for sizes in pieces]
    carried = grads[1][0] if len(pieces) == 2 else None
    held, total, turned, active, blocks, b, h, here, arrived = refs
    emb = grads[0][0].shape[1]
    slots = blocks.shape[1]
    tile = held.shape[1]
    wanted = [b, h] + [blocks.at[k] for k in range(len(pieces))]
    small = [
        pltpu.make_async_copy(source, goal, here.at[i])
        for i, (source, goal) in enumerate(zip(given[1:], wanted))
    ]
    for copy in small:
        copy.start()

    def fetch(i):
        cut = part_of(i, tile)
        return pltpu.make_async_copy(given[0].at[:, cut], w.at[:, cut], arrived.at[i])

    @pl.loop(0, w.shape[1] // tile)
    def _(i):
        fetch(i).start()

    for copy in small:
        copy.wait()
    copy_features(slot_of, [[blocks.at[k]] for k in range(len(pieces))], feats)
    total[...] = jnp.zeros_like(total)

    def finish(i, pre):
        cut = part_of(i, pre.shape[1])
        head = h[:, cut].astype(jnp.float32)
        sigmoid, act = swish(pre)
        add_lanes(total, act * head)
        low = (head * (sigmoid + act * (1.0 - sigmoid))).astype(jnp.bfloat16)
        slope[:, cut] = low
        turned[cut, :] = low.T
        active[:, cut] = act.astype(jnp.bfloat16)

    forward_tiles(feats, w, b, held, finish, lambda i: fetch(i).wait())
    logit[...] = jnp.sum(total[...].T, axis=0, keepdims=True)

    keep = pltpu.make_async_copy(active, active_out, here.at[len(small)])
    keep.start()
    for grad in sum(grads, []):
        grad[...] = jnp.zeros_like(grad)
    if carried is not None:
        carried[carried.shape[0] - 1, :16, :] = in_terms(logit[...])

    me, tables = lax.axis_index("table"), lax.axis_size("table")
    used = w.shape[0] // emb
    group = max(n for n in range(1, 14) if used % n == 0)

    @pl.loop(0, used // group)
    def _(i):
        value = jnp.dot(
            w[part_of(i, group * emb), :], turned[...], preferred_element_type=jnp.float32
        ).astype(jnp.bfloat16)
        for j in range(group):
            slot = slot_of[group * i + j]
            owner = lax.rem(slot // slots + tables - me, tables)
            place = lax.rem(slot, slots)
            for k in range(len(grads)):
                first = 0
                for grad, size in zip(grads[k], pieces[k]):
                    last = first + size

                    @pl.when((owner == k) & (place >= first) & (place < last))
                    def _():
                        grad[place - first] = value[j * emb : (j + 1) * emb, :]

                    first = last

    keep.wait()


def student(slot_of, blocks, w, b, h):
    slots, rows, emb = blocks[0].shape
    depth, units = w.shape
    first = (3 * slots) // 7
    sizes = [first, slots - first] if len(blocks) == 2 else [slots]
    pieces = [[slots]] + [sizes] * (len(blocks) - 1)
    shape = jax.ShapeDtypeStruct
    given = [in_hbm(value) for value in (w, b, h, blocks[0])] + blocks[1:]
    results = pl.pallas_call(
        functools.partial(student_body, pieces),
        in_specs=[SMEM] + [HBM] * 4 + [pl.BlockSpec(memory_space=pl.ANY)] * (len(given) - 4),
        out_specs=[VMEM, VMEM, HBM] + [VMEM] * (2 + sum(len(sizes) for sizes in pieces)),
        out_shape=[
            shape((1, rows), jnp.float32),
            shape((rows, units), jnp.bfloat16),
            pltpu.HBM((rows, units), jnp.bfloat16),
            shape((rows, depth), jnp.bfloat16),
            shape((depth, units), jnp.bfloat16),
        ]
        + [
            shape((size + (len(blocks) == 2 and (k, j) == (1, 0)), emb, rows), jnp.bfloat16)
            for k, sizes in enumerate(pieces)
            for j, size in enumerate(sizes)
        ],
        scratch_shapes=[
            pltpu.VMEM((rows, tiles(units)), jnp.float32),
            pltpu.VMEM((rows, 128), jnp.float32),
            pltpu.VMEM((units, rows), jnp.bfloat16),
            pltpu.VMEM((rows, units), jnp.bfloat16),
            pltpu.VMEM((len(blocks), slots, rows, emb), jnp.bfloat16),
            pltpu.VMEM((1, units), jnp.bfloat16),
            pltpu.VMEM((1, units), jnp.bfloat16),
            pltpu.SemaphoreType.DMA((3 + len(blocks),)),
            pltpu.SemaphoreType.DMA((units // tiles(units),)),
        ],
        compiler_params=pltpu.CompilerParams(vmem_limit_bytes=VMEM_LIMIT),
        cost_estimate=pl.CostEstimate(
            flops=4 * rows * depth * units,
            bytes_accessed=2 * depth * units,
            transcendentals=rows * units,
        ),
    )(slot_of, *given)
    grads = list(results[5:])
    return *results[:5], [[grads.pop(0) for _ in sizes] for sizes in pieces]


def teacher_body(pieces, slot_of, *refs):
    count = sum(pieces)
    blocks, (w, b, h, logit, feats, held, total) = list(refs[:count]), refs[count:]
    copy_features(slot_of, [[blocks.pop(0) for _ in range(n)] for n in pieces], feats)
    total[...] = jnp.zeros_like(total)

    def finish(i, pre):
        head = h[:, part_of(i, pre.shape[1])].astype(jnp.float32)
        add_lanes(total, swish(pre)[1] * head)

    forward_tiles(feats, w, b, held, finish)
    logit[...] = jnp.sum(total[...].T, axis=0, keepdims=True)


def teacher(slot_of, blocks, w, b, h):
    rows = blocks[0][0].shape[1]
    depth, units = w.shape
    pieces = [len(block) for block in blocks]
    count = sum(pieces)
    return pl.pallas_call(
        functools.partial(teacher_body, pieces),
        in_specs=[SMEM] + [VMEM] * (count + 3),
        out_specs=VMEM,
        out_shape=jax.ShapeDtypeStruct((1, rows), jnp.float32),
        scratch_shapes=[
            pltpu.VMEM((rows, depth), jnp.bfloat16),
            pltpu.VMEM((rows, tiles(units)), jnp.float32),
            pltpu.VMEM((rows, 128), jnp.float32),
        ],
        compiler_params=pltpu.CompilerParams(vmem_limit_bytes=VMEM_LIMIT),
        cost_estimate=pl.CostEstimate(
            flops=2 * rows * depth * units,
            bytes_accessed=2 * depth * units,
            transcendentals=rows * units,
        ),
    )(slot_of, *(piece for block in blocks for piece in block), w, b, h)


def rows_body(count, y_ref, *refs):
    zs, ts, refs = refs[:count], refs[count : 2 * count], refs[2 * count :]
    slope, active_in, low, bias, head, loss, scale, active, here = refs
    rows = y_ref.shape[1]
    fetch = pltpu.make_async_copy(active_in, active, here)
    fetch.start()
    z = zs[0][...]
    if count == 2:
        z = z + from_terms(zs[1][zs[1].shape[0] - 1, :16, :])
    soft = jax.nn.sigmoid(sum(ref[...] for ref in ts))
    y = y_ref[...].astype(jnp.float32)
    grads = 2.0 * jax.nn.sigmoid(z) - y - soft
    scale[...] = grads
    softplus = jnp.maximum(z, 0.0) + jnp.log1p(jnp.exp(-jnp.abs(z)))
    losses = 2.0 * softplus - y * z - soft * z
    loss[...] = jnp.sum(losses, axis=1, keepdims=True) / rows
    column = jnp.broadcast_to(grads, (128, rows)).T

    @pl.loop(0, slope.shape[1] // 512)
    def _(i):
        for j in range(4):
            cut = part_of(4 * i + j, 128)
            pre = slope[:, cut].astype(jnp.float32) * column
            low[:, cut] = pre.astype(jnp.bfloat16)
            bias[:, cut] = jnp.sum(pre, axis=0, keepdims=True)

    fetch.wait()

    @pl.loop(0, slope.shape[1] // 512)
    def _(i):
        for j in range(4):
            cut = part_of(4 * i + j, 128)
            head[:, cut] = jnp.sum(
                active[:, cut].astype(jnp.float32) * column, axis=0, keepdims=True
            )


def row_grads(z_parts, t_parts, labels, slope, active):
    rows, units = slope.shape
    shape = jax.ShapeDtypeStruct
    row, units_row = whole((1, rows)), whole((1, units))
    return pl.pallas_call(
        functools.partial(rows_body, len(z_parts)),
        grid=(1,),
        in_specs=[row] * 2 + [VMEM] * (len(z_parts) - 1) + [row] * len(t_parts) + [VMEM, HBM],
        out_specs=[VMEM, units_row, units_row, whole((1, 1)), row],
        out_shape=[
            shape((rows, units), jnp.bfloat16),
            shape((1, units), jnp.float32),
            shape((1, units), jnp.float32),
            shape((1, 1), jnp.float32),
            shape((1, rows), jnp.float32),
        ],
        scratch_shapes=[pltpu.VMEM((rows, units), jnp.bfloat16), pltpu.SemaphoreType.DMA],
        compiler_params=pltpu.CompilerParams(vmem_limit_bytes=VMEM_LIMIT),
    )(in_hbm(labels), *z_parts, *t_parts, slope, in_hbm(active))


def scaled_body(sizes, scale, kept, *refs):
    others, out = refs[:-1], refs[-1]
    factor, first = scale[...], 0
    for i, size in enumerate(sizes):
        cut = slice(first, first + size)
        total = kept[cut].astype(jnp.float32)
        for piece in others[i :: len(sizes)]:
            total = total + piece[:size].astype(jnp.float32)
        out[cut] = (total * factor).astype(jnp.bfloat16)
        first += size


def scaled_sum(scale, kept, others):
    slots, emb, rows = kept.shape
    last = [piece.shape[0] for piece in others[0][1:]]
    sizes = [slots - sum(last)] + last
    flat = [piece for pieces in others for piece in pieces]
    return pl.pallas_call(
        functools.partial(scaled_body, sizes),
        in_specs=[VMEM] * (2 + len(flat)),
        out_specs=VMEM,
        out_shape=jax.ShapeDtypeStruct((slots, emb, rows), jnp.bfloat16),
        compiler_params=pltpu.CompilerParams(vmem_limit_bytes=VMEM_LIMIT),
    )(scale.reshape(1, 1, rows), kept, *flat)


def across(value, shift):
    count = lax.axis_size("table")
    return lax.ppermute(value, "table", [(i, (i + shift) % count) for i in range(count)])


def swap(bits, value, shift=0):
    copies, tables = lax.axis_size("copy"), lax.axis_size("table")
    pairs = [
        (c * tables + i, (c ^ bits) * tables + (i + shift) % tables)
        for c in range(copies)
        for i in range(tables)
    ]
    return lax.ppermute(value, ("copy", "table"), pairs)


def after(value, other):
    return lax.optimization_barrier((value, other))[0]


def by_distance(run, distance, *values):
    branches = [functools.partial(run, bits) for bits in range(1, lax.axis_size("copy"))]
    return lax.switch(distance - 1, branches, *values)


def swap_rows(bits, own):
    cut = (2 * own.shape[0]) // 7
    first = swap(bits, own[:cut])
    second = swap(bits, after(own[cut:], first))
    return across(own, 1), first, second, across(first, 1)


def swap_logits(bits, t_own):
    return swap(bits, t_own), swap(bits, t_own, 1)


def on_device(pooled, slot_of_table, partner, labels, w_first, b_first, w_head):
    tables = lax.axis_size("table")
    rows, slots, emb = pooled.shape
    me_copy = lax.axis_index("copy")
    distance = jnp.bitwise_xor(me_copy, partner[me_copy])

    own = jnp.transpose(pooled, (1, 0, 2))
    if tables == 2:
        other, first, second, first_other = by_distance(swap_rows, distance, own)
        blocks = [own, other]
        their_blocks = [[first, second], [first_other, across(second, 1)]]
    else:
        blocks = [own] + [across(own, k) for k in range(1, tables)]
        theirs = by_distance(swap, distance, own)
        their_blocks = [[theirs]] + [[across(theirs, k)] for k in range(1, tables)]

    z_own, slope, active, feats, w, grads = student(
        slot_of_table, blocks, w_first[0], b_first, w_head
    )
    early = [across(pieces[0], k) for k, pieces in enumerate(grads) if k]
    t_own = teacher(slot_of_table, their_blocks, w, b_first, w_head)
    for piece in early:
        t_own = after(t_own, piece)
    if tables == 2:
        t_parts = by_distance(swap_logits, distance, t_own)
        z_parts = [z_own, early[0]]
    else:
        z_own, t_own = lax.psum((z_own, t_own), "table")
        z_parts, t_parts = [z_own], [by_distance(swap, distance, t_own)]
    others = [
        [piece] + [across(after(rest, t_parts[-1]), k) for rest in grads[k][1:]]
        for k, piece in enumerate(early, 1)
    ]

    low, grad_bias, grad_head, loss, scale = row_grads(
        z_parts, t_parts, labels.reshape(1, rows), slope, active
    )
    grad_first = lax.dot_general(
        feats, low, (((0,), (0,)), ((), ())), preferred_element_type=jnp.float32
    ).astype(jnp.bfloat16)
    pooled_grad = scaled_sum(scale, grads[0][0], others)
    return (pooled_grad, grad_first[None], grad_bias, grad_head, loss.reshape(1))


def solution(mesh):
    in_specs = (
        P("copy", "table", None),
        P(),
        P(),
        P("copy"),
        P("copy", None, "table"),
        P("copy", "table"),
        P("copy", "table"),
    )
    out_specs = (
        P("table", None, "copy"),
        P("copy", None, "table"),
        P("copy", "table"),
        P("copy", "table"),
        P("copy"),
    )
    return jax.shard_map(
        on_device, mesh=mesh, in_specs=in_specs, out_specs=out_specs, check_vma=False
    )
```

```python
import functools

import jax
import jax.numpy as jnp
from jax import lax
from jax.experimental import pallas as pl
from jax.experimental.pallas import tpu as pltpu
from jax.sharding import PartitionSpec as P

VMEM_LIMIT = 12 * 1024 * 1024
VMEM = pl.BlockSpec(memory_space=pltpu.VMEM)
SMEM = pl.BlockSpec(memory_space=pltpu.SMEM)
HBM = pl.BlockSpec(memory_space=pltpu.HBM)
TILE = 256


def in_hbm(value):
    return pltpu.with_memory_space_constraint(value, pltpu.HBM)


def whole(shape):
    return pl.BlockSpec(shape, lambda *_: (0,) * len(shape))


def tiles(width):
    return TILE if width % TILE == 0 else width


def part_of(i, size):
    return pl.ds(pl.multiple_of(i * size, size), size)


def copy_features(slot_of, blocks, feats):
    me = lax.axis_index("table")
    tables, slots, _, emb = blocks.shape

    @pl.loop(0, feats.shape[1] // emb)
    def _(t):
        slot = slot_of[t]
        group = lax.rem(me + tables - slot // slots, tables)
        feats[:, part_of(t, emb)] = blocks[group, lax.rem(slot, slots)]


def forward_tiles(feats, w, b, held, finish, arrive=lambda i: None):
    tile = held.shape[1]
    count = w.shape[1] // tile

    def product(i):
        arrive(i)
        cut = part_of(i, tile)
        value = jnp.dot(feats[...], w[:, cut], preferred_element_type=jnp.float32)
        return value + b[:, cut].astype(jnp.float32)

    held[...] = product(0)

    @pl.loop(1, count)
    def _(i):
        before = held[...]
        value = product(i)
        finish(i - 1, before)
        held[...] = value

    finish(count - 1, held[...])


def swish(pre):
    sigmoid = 0.5 * jnp.tanh(0.5 * pre) + 0.5
    return sigmoid, pre * sigmoid


def add_lanes(total, wide):
    for lane in range(0, wide.shape[1], 128):
        total[...] += wide[:, lane : lane + 128]


def in_terms(row):
    high = row.astype(jnp.bfloat16).astype(jnp.float32)
    middle = (row - high).astype(jnp.bfloat16).astype(jnp.float32)
    at = lax.broadcasted_iota(jnp.int32, (16, row.shape[1]), 0)
    terms = jnp.where(at == 0, high, jnp.where(at == 1, middle, row - high - middle))
    return terms.astype(jnp.bfloat16)


def from_terms(terms):
    wide = terms.astype(jnp.float32)
    return wide[0:1] + wide[1:2] + wide[2:3]


def student_body(pieces, slot_of, *refs):
    given, refs = refs[: 3 + len(pieces)], refs[3 + len(pieces) :]
    logit, slope, active_out, feats, w, *refs = refs
    grads = [[refs.pop(0) for _ in sizes] for sizes in pieces]
    carried = grads[1][0] if len(pieces) == 2 else None
    held, total, turned, active, every, blocks, b, h, here, arrived = refs
    emb = grads[0][0].shape[1]
    slots = blocks.shape[1]
    tile = held.shape[1]
    wanted = [b, h] + [blocks.at[k] for k in range(len(pieces))]
    small = [
        pltpu.make_async_copy(source, goal, here.at[i])
        for i, (source, goal) in enumerate(zip(given[1:], wanted))
    ]
    for copy in small:
        copy.start()

    def fetch(i):
        cut = part_of(i, tile)
        return pltpu.make_async_copy(given[0].at[:, cut], w.at[:, cut], arrived.at[i])

    @pl.loop(0, w.shape[1] // tile)
    def _(i):
        fetch(i).start()

    for copy in small:
        copy.wait()
    copy_features(slot_of, blocks, feats)
    total[...] = jnp.zeros_like(total)

    def finish(i, pre):
        cut = part_of(i, pre.shape[1])
        head = h[:, cut].astype(jnp.float32)
        sigmoid, act = swish(pre)
        add_lanes(total, act * head)
        low = (head * (sigmoid + act * (1.0 - sigmoid))).astype(jnp.bfloat16)
        slope[:, cut] = low
        turned[cut, :] = low.T
        active[:, cut] = act.astype(jnp.bfloat16)

    forward_tiles(feats, w, b, held, finish, lambda i: fetch(i).wait())
    logit[...] = jnp.sum(total[...].T, axis=0, keepdims=True)

    keep = pltpu.make_async_copy(active, active_out, here.at[len(small)])
    keep.start()
    every[...] = jnp.zeros_like(every)
    if carried is not None:
        extra = carried.shape[0] - 1
        carried[extra] = jnp.zeros(carried.shape[1:], carried.dtype)
        carried[extra, :16, :] = in_terms(logit[...])

    me, tables = lax.axis_index("table"), lax.axis_size("table")
    used = w.shape[0] // emb
    group = max(n for n in range(1, 14) if used % n == 0)

    @pl.loop(0, used // group)
    def _(i):
        value = jnp.dot(
            w[part_of(i, group * emb), :], turned[...], preferred_element_type=jnp.float32
        ).astype(jnp.bfloat16)
        for j in range(group):
            slot = slot_of[group * i + j]
            owner = lax.rem(slot // slots + tables - me, tables)
            every[owner * slots + lax.rem(slot, slots)] = value[j * emb : (j + 1) * emb, :]

    kept = pltpu.make_async_copy(every.at[:slots], grads[0][0], here.at[len(small) + 1])
    kept.start()
    for k in range(1, len(pieces)):
        first = k * slots
        for grad, size in zip(grads[k], pieces[k]):
            grad[:size] = every[first : first + size]
            first += size

    kept.wait()
    keep.wait()


def student(slot_of, blocks, w, b, h):
    slots, rows, emb = blocks[0].shape
    depth, units = w.shape
    first = (3 * slots) // 7
    sizes = [first, slots - first] if len(blocks) == 2 else [slots]
    pieces = [[slots]] + [sizes] * (len(blocks) - 1)
    shape = jax.ShapeDtypeStruct
    given = [in_hbm(value) for value in (w, b, h, blocks[0])] + blocks[1:]
    results = pl.pallas_call(
        functools.partial(student_body, pieces),
        in_specs=[SMEM] + [HBM] * 4 + [pl.BlockSpec(memory_space=pl.ANY)] * (len(given) - 4),
        out_specs=[VMEM, VMEM, HBM, VMEM, VMEM, HBM]
        + [VMEM] * sum(len(sizes) for sizes in pieces[1:]),
        out_shape=[
            shape((1, rows), jnp.float32),
            shape((rows, units), jnp.bfloat16),
            pltpu.HBM((rows, units), jnp.bfloat16),
            shape((rows, depth), jnp.bfloat16),
            shape((depth, units), jnp.bfloat16),
        ]
        + [pltpu.HBM((slots, emb, rows), jnp.bfloat16)]
        + [
            shape((size + (len(blocks) == 2 and j == 0), emb, rows), jnp.bfloat16)
            for sizes in pieces[1:]
            for j, size in enumerate(sizes)
        ],
        scratch_shapes=[
            pltpu.VMEM((rows, tiles(units)), jnp.float32),
            pltpu.VMEM((rows, 128), jnp.float32),
            pltpu.VMEM((units, rows), jnp.bfloat16),
            pltpu.VMEM((rows, units), jnp.bfloat16),
            pltpu.VMEM((len(blocks) * slots, emb, rows), jnp.bfloat16),
            pltpu.VMEM((len(blocks), slots, rows, emb), jnp.bfloat16),
            pltpu.VMEM((1, units), jnp.bfloat16),
            pltpu.VMEM((1, units), jnp.bfloat16),
            pltpu.SemaphoreType.DMA((4 + len(blocks),)),
            pltpu.SemaphoreType.DMA((units // tiles(units),)),
        ],
        compiler_params=pltpu.CompilerParams(vmem_limit_bytes=VMEM_LIMIT),
        cost_estimate=pl.CostEstimate(
            flops=4 * rows * depth * units,
            bytes_accessed=2 * depth * units,
            transcendentals=rows * units,
        ),
    )(slot_of, *given)
    grads = list(results[5:])
    return *results[:5], [[grads.pop(0) for _ in sizes] for sizes in pieces]


def teacher_body(pieces, slot_of, *refs):
    count = sum(pieces)
    sources, (w, b, h, logit, feats, blocks, held, total, here) = list(refs[:count]), refs[count:]
    copies = []
    for k, n in enumerate(pieces):
        first = 0
        for _ in range(n):
            source = sources.pop(0)
            last = first + source.shape[0]
            copies.append(
                pltpu.make_async_copy(source, blocks.at[k, first:last], here.at[len(copies)])
            )
            first = last
    for copy in copies:
        copy.start()
    for copy in copies:
        copy.wait()
    copy_features(slot_of, blocks, feats)
    total[...] = jnp.zeros_like(total)

    def finish(i, pre):
        head = h[:, part_of(i, pre.shape[1])].astype(jnp.float32)
        add_lanes(total, swish(pre)[1] * head)

    forward_tiles(feats, w, b, held, finish)
    logit[...] = jnp.sum(total[...].T, axis=0, keepdims=True)


def teacher(slot_of, blocks, w, b, h):
    _, rows, emb = blocks[0][0].shape
    slots = sum(piece.shape[0] for piece in blocks[0])
    depth, units = w.shape
    pieces = [len(block) for block in blocks]
    count = sum(pieces)
    return pl.pallas_call(
        functools.partial(teacher_body, pieces),
        in_specs=[SMEM] + [pl.BlockSpec(memory_space=pl.ANY)] * count + [VMEM] * 3,
        out_specs=VMEM,
        out_shape=jax.ShapeDtypeStruct((1, rows), jnp.float32),
        scratch_shapes=[
            pltpu.VMEM((rows, depth), jnp.bfloat16),
            pltpu.VMEM((len(blocks), slots, rows, emb), jnp.bfloat16),
            pltpu.VMEM((rows, tiles(units)), jnp.float32),
            pltpu.VMEM((rows, 128), jnp.float32),
            pltpu.SemaphoreType.DMA((count,)),
        ],
        compiler_params=pltpu.CompilerParams(vmem_limit_bytes=VMEM_LIMIT),
        cost_estimate=pl.CostEstimate(
            flops=2 * rows * depth * units,
            bytes_accessed=2 * depth * units,
            transcendentals=rows * units,
        ),
    )(slot_of, *(piece for block in blocks for piece in block), w, b, h)


def rows_body(count, y_ref, *refs):
    zs, ts, refs = refs[:count], refs[count : 2 * count], refs[2 * count :]
    slope, active_in, low, bias, head, loss, scale, active, here = refs
    rows = y_ref.shape[1]
    fetch = pltpu.make_async_copy(active_in, active, here)
    fetch.start()
    z = zs[0][...]
    if count == 2:
        z = z + from_terms(zs[1][zs[1].shape[0] - 1, :16, :])
    soft = jax.nn.sigmoid(sum(ref[...] for ref in ts))
    y = y_ref[...].astype(jnp.float32)
    grads = 2.0 * jax.nn.sigmoid(z) - y - soft
    scale[...] = grads
    softplus = jnp.maximum(z, 0.0) + jnp.log1p(jnp.exp(-jnp.abs(z)))
    losses = 2.0 * softplus - y * z - soft * z
    loss[...] = jnp.sum(losses, axis=1, keepdims=True) / rows
    column = jnp.broadcast_to(grads, (128, rows)).T

    @pl.loop(0, slope.shape[1] // 512)
    def _(i):
        for j in range(4):
            cut = part_of(4 * i + j, 128)
            pre = slope[:, cut].astype(jnp.float32) * column
            low[:, cut] = pre.astype(jnp.bfloat16)
            bias[:, cut] = jnp.sum(pre, axis=0, keepdims=True)

    fetch.wait()

    @pl.loop(0, slope.shape[1] // 512)
    def _(i):
        for j in range(4):
            cut = part_of(4 * i + j, 128)
            head[:, cut] = jnp.sum(
                active[:, cut].astype(jnp.float32) * column, axis=0, keepdims=True
            )


def row_grads(z_parts, t_parts, labels, slope, active):
    rows, units = slope.shape
    shape = jax.ShapeDtypeStruct
    row, units_row = whole((1, rows)), whole((1, units))
    return pl.pallas_call(
        functools.partial(rows_body, len(z_parts)),
        grid=(1,),
        in_specs=[row] * 2 + [VMEM] * (len(z_parts) - 1) + [row] * len(t_parts) + [VMEM, HBM],
        out_specs=[VMEM, units_row, units_row, whole((1, 1)), row],
        out_shape=[
            shape((rows, units), jnp.bfloat16),
            shape((1, units), jnp.float32),
            shape((1, units), jnp.float32),
            shape((1, 1), jnp.float32),
            shape((1, rows), jnp.float32),
        ],
        scratch_shapes=[pltpu.VMEM((rows, units), jnp.bfloat16), pltpu.SemaphoreType.DMA],
        compiler_params=pltpu.CompilerParams(vmem_limit_bytes=VMEM_LIMIT),
    )(in_hbm(labels), *z_parts, *t_parts, slope, in_hbm(active))


def scaled_body(sizes, scale, kept, *refs):
    others, out = refs[:-1], refs[-1]
    factor, first = scale[...], 0
    for i, size in enumerate(sizes):
        cut = slice(first, first + size)
        total = kept[cut].astype(jnp.float32)
        for piece in others[i :: len(sizes)]:
            total = total + piece[:size].astype(jnp.float32)
        out[cut] = (total * factor).astype(jnp.bfloat16)
        first += size


def scaled_sum(scale, kept, others):
    slots, emb, rows = kept.shape
    last = [piece.shape[0] for piece in others[0][1:]]
    sizes = [slots - sum(last)] + last
    flat = [piece for pieces in others for piece in pieces]
    return pl.pallas_call(
        functools.partial(scaled_body, sizes),
        in_specs=[VMEM] * (2 + len(flat)),
        out_specs=VMEM,
        out_shape=jax.ShapeDtypeStruct((slots, emb, rows), jnp.bfloat16),
        compiler_params=pltpu.CompilerParams(vmem_limit_bytes=VMEM_LIMIT),
    )(scale.reshape(1, 1, rows), kept, *flat)


def across(value, shift):
    count = lax.axis_size("table")
    return lax.ppermute(value, "table", [(i, (i + shift) % count) for i in range(count)])


def swap(bits, value, shift=0):
    copies, tables = lax.axis_size("copy"), lax.axis_size("table")
    pairs = [
        (c * tables + i, (c ^ bits) * tables + (i + shift) % tables)
        for c in range(copies)
        for i in range(tables)
    ]
    return lax.ppermute(value, ("copy", "table"), pairs)


def after(value, other):
    return lax.optimization_barrier((value, other))[0]


def by_distance(run, distance, *values):
    branches = [functools.partial(run, bits) for bits in range(1, lax.axis_size("copy"))]
    return lax.switch(distance - 1, branches, *values)


def swap_rows(bits, own):
    cut = (2 * own.shape[0]) // 7
    first = swap(bits, own[:cut])
    second = swap(bits, after(own[cut:], first))
    return across(own, 1), first, second, across(first, 1)


def swap_logits(bits, t_own):
    return swap(bits, t_own), swap(bits, t_own, 1)


def on_device(pooled, slot_of_table, partner, labels, w_first, b_first, w_head):
    tables = lax.axis_size("table")
    rows, slots, emb = pooled.shape
    me_copy = lax.axis_index("copy")
    distance = jnp.bitwise_xor(me_copy, partner[me_copy])

    own = jnp.transpose(pooled, (1, 0, 2))
    if tables == 2:
        other, first, second, first_other = by_distance(swap_rows, distance, own)
        blocks = [own, other]
        their_blocks = [[first, second], [first_other, across(second, 1)]]
    else:
        blocks = [own] + [across(own, k) for k in range(1, tables)]
        theirs = by_distance(swap, distance, own)
        their_blocks = [[theirs]] + [[across(theirs, k)] for k in range(1, tables)]

    z_own, slope, active, feats, w, grads = student(
        slot_of_table, blocks, w_first[0], b_first, w_head
    )
    early = [across(pieces[0], k) for k, pieces in enumerate(grads) if k]
    t_own = teacher(slot_of_table, their_blocks, w, b_first, w_head)
    for piece in early:
        t_own = after(t_own, piece)
    if tables == 2:
        t_parts = by_distance(swap_logits, distance, t_own)
        z_parts = [z_own, early[0]]
    else:
        z_own, t_own = lax.psum((z_own, t_own), "table")
        z_parts, t_parts = [z_own], [by_distance(swap, distance, t_own)]
    others = [
        [piece] + [across(after(rest, t_parts[-1]), k) for rest in grads[k][1:]]
        for k, piece in enumerate(early, 1)
    ]

    low, grad_bias, grad_head, loss, scale = row_grads(
        z_parts, t_parts, labels.reshape(1, rows), slope, active
    )
    grad_first = lax.dot_general(
        feats, low, (((0,), (0,)), ((), ())), preferred_element_type=jnp.float32
    ).astype(jnp.bfloat16)
    pooled_grad = scaled_sum(scale, grads[0][0], others)
    return (pooled_grad, grad_first[None], grad_bias, grad_head, loss.reshape(1))


def solution(mesh):
    in_specs = (
        P("copy", "table", None),
        P(),
        P(),
        P("copy"),
        P("copy", None, "table"),
        P("copy", "table"),
        P("copy", "table"),
    )
    out_specs = (
        P("table", None, "copy"),
        P("copy", None, "table"),
        P("copy", "table"),
        P("copy", "table"),
        P("copy"),
    )
    return jax.shard_map(
        on_device, mesh=mesh, in_specs=in_specs, out_specs=out_specs, check_vma=False
    )
```

```python
import functools

import jax
import jax.numpy as jnp
from jax import lax
from jax.experimental import pallas as pl
from jax.experimental.pallas import tpu as pltpu
from jax.sharding import PartitionSpec as P

VMEM_LIMIT = 12 * 1024 * 1024
VMEM = pl.BlockSpec(memory_space=pltpu.VMEM)
SMEM = pl.BlockSpec(memory_space=pltpu.SMEM)
HBM = pl.BlockSpec(memory_space=pltpu.HBM)
TILE = 256


def in_hbm(value):
    return pltpu.with_memory_space_constraint(value, pltpu.HBM)


def whole(shape):
    return pl.BlockSpec(shape, lambda *_: (0,) * len(shape))


def tiles(width):
    return TILE if width % TILE == 0 else width


def part_of(i, size):
    return pl.ds(pl.multiple_of(i * size, size), size)


def copy_features(slot_of, blocks, feats):
    me = lax.axis_index("table")
    tables, slots, _, emb = blocks.shape

    @pl.loop(0, feats.shape[1] // emb)
    def _(t):
        slot = slot_of[t]
        group = lax.rem(me + tables - slot // slots, tables)
        feats[:, part_of(t, emb)] = blocks[group, lax.rem(slot, slots)]


def forward_tiles(feats, w, b, held, finish):
    tile = held.shape[1]
    count = w.shape[1] // tile

    def product(i):
        cut = part_of(i, tile)
        value = jnp.dot(feats[...], w[:, cut], preferred_element_type=jnp.float32)
        return value + b[:, cut].astype(jnp.float32)

    held[...] = product(0)

    @pl.loop(1, count)
    def _(i):
        before = held[...]
        value = product(i)
        finish(i - 1, before)
        held[...] = value

    finish(count - 1, held[...])


def swish(pre):
    sigmoid = 0.5 * jnp.tanh(0.5 * pre) + 0.5
    return sigmoid, pre * sigmoid


def add_lanes(total, wide):
    for lane in range(0, wide.shape[1], 128):
        total[...] += wide[:, lane : lane + 128]


def in_terms(row):
    high = row.astype(jnp.bfloat16).astype(jnp.float32)
    middle = (row - high).astype(jnp.bfloat16).astype(jnp.float32)
    at = lax.broadcasted_iota(jnp.int32, (16, row.shape[1]), 0)
    terms = jnp.where(at == 0, high, jnp.where(at == 1, middle, row - high - middle))
    return terms.astype(jnp.bfloat16)


def from_terms(terms):
    wide = terms.astype(jnp.float32)
    return wide[0:1] + wide[1:2] + wide[2:3]


def load_body(source, goal, here):
    copy = pltpu.make_async_copy(source, goal, here)
    copy.start()
    copy.wait()


def in_vmem(value):
    return pl.pallas_call(
        load_body,
        in_specs=[HBM],
        out_specs=VMEM,
        out_shape=jax.ShapeDtypeStruct(value.shape, value.dtype),
        scratch_shapes=[pltpu.SemaphoreType.DMA],
        compiler_params=pltpu.CompilerParams(vmem_limit_bytes=1024 * 1024),
    )(in_hbm(value))


def features_body(slot_of, *refs):
    sources, (feats, again, blocks, here) = refs[:-4], refs[-4:]
    copies = [
        pltpu.make_async_copy(source, blocks.at[k], here.at[k])
        for k, source in enumerate(sources)
    ]
    for copy in copies:
        copy.start()
    for copy in copies:
        copy.wait()
    copy_features(slot_of, blocks, feats)
    again[...] = feats[...]


def features(slot_of, blocks):
    slots, rows, emb = blocks[0].shape
    depth = slot_of.shape[0] * emb
    return pl.pallas_call(
        features_body,
        in_specs=[SMEM] + [pl.BlockSpec(memory_space=pl.ANY)] * len(blocks),
        out_specs=[VMEM] * 2,
        out_shape=[jax.ShapeDtypeStruct((rows, depth), jnp.bfloat16)] * 2,
        scratch_shapes=[
            pltpu.VMEM((len(blocks), slots, rows, emb), jnp.bfloat16),
            pltpu.SemaphoreType.DMA((len(blocks),)),
        ],
        compiler_params=pltpu.CompilerParams(vmem_limit_bytes=6 * 1024 * 1024),
    )(slot_of, *blocks)


def student_body(pieces, slot_of, *refs):
    feats, w, b_in, h_in, logit, slope, active_out, *refs = refs
    grads = [[refs.pop(0) for _ in sizes] for sizes in pieces]
    carried = grads[1][0] if len(pieces) == 2 else None
    held, total, turned, active, every, b, h, here = refs
    emb = grads[0][0].shape[1]
    slots = grads[0][0].shape[0]
    small = [
        pltpu.make_async_copy(b_in, b, here.at[0]),
        pltpu.make_async_copy(h_in, h, here.at[1]),
    ]
    for copy in small:
        copy.start()
    for copy in small:
        copy.wait()
    total[...] = jnp.zeros_like(total)

    def finish(i, pre):
        cut = part_of(i, pre.shape[1])
        head = h[:, cut].astype(jnp.float32)
        sigmoid, act = swish(pre)
        add_lanes(total, act * head)
        low = (head * (sigmoid + act * (1.0 - sigmoid))).astype(jnp.bfloat16)
        slope[:, cut] = low
        turned[cut, :] = low.T
        active[:, cut] = act.astype(jnp.bfloat16)

    forward_tiles(feats, w, b, held, finish)
    logit[...] = jnp.sum(total[...].T, axis=0, keepdims=True)

    keep = pltpu.make_async_copy(active, active_out, here.at[len(small)])
    keep.start()
    every[...] = jnp.zeros_like(every)
    if carried is not None:
        extra = carried.shape[0] - 1
        carried[extra] = jnp.zeros(carried.shape[1:], carried.dtype)
        carried[extra, :16, :] = in_terms(logit[...])

    me, tables = lax.axis_index("table"), lax.axis_size("table")
    used = w.shape[0] // emb
    group = max(n for n in range(1, 14) if used % n == 0)

    @pl.loop(0, used // group)
    def _(i):
        value = jnp.dot(
            w[part_of(i, group * emb), :], turned[...], preferred_element_type=jnp.float32
        ).astype(jnp.bfloat16)
        for j in range(group):
            slot = slot_of[group * i + j]
            owner = lax.rem(slot // slots + tables - me, tables)
            every[owner * slots + lax.rem(slot, slots)] = value[j * emb : (j + 1) * emb, :]

    kept = pltpu.make_async_copy(every.at[:slots], grads[0][0], here.at[len(small) + 1])
    kept.start()
    for k in range(1, len(pieces)):
        first = k * slots
        for grad, size in zip(grads[k], pieces[k]):
            grad[:size] = every[first : first + size]
            first += size

    kept.wait()
    keep.wait()


def student(slot_of, feats, w, b, h, slots):
    rows, depth = feats.shape
    units = w.shape[1]
    emb = depth // slot_of.shape[0]
    tables = lax.axis_size("table")
    first = (3 * slots) // 7
    sizes = [first, slots - first] if tables == 2 else [slots]
    pieces = [[slots]] + [sizes] * (tables - 1)
    shape = jax.ShapeDtypeStruct
    results = pl.pallas_call(
        functools.partial(student_body, pieces),
        in_specs=[SMEM, VMEM, VMEM, HBM, HBM],
        out_specs=[VMEM, VMEM, HBM, HBM] + [VMEM] * sum(len(sizes) for sizes in pieces[1:]),
        out_shape=[
            shape((1, rows), jnp.float32),
            shape((rows, units), jnp.bfloat16),
            pltpu.HBM((rows, units), jnp.bfloat16),
            pltpu.HBM((slots, emb, rows), jnp.bfloat16),
        ]
        + [
            shape((size + (tables == 2 and j == 0), emb, rows), jnp.bfloat16)
            for sizes in pieces[1:]
            for j, size in enumerate(sizes)
        ],
        scratch_shapes=[
            pltpu.VMEM((rows, tiles(units)), jnp.float32),
            pltpu.VMEM((rows, 128), jnp.float32),
            pltpu.VMEM((units, rows), jnp.bfloat16),
            pltpu.VMEM((rows, units), jnp.bfloat16),
            pltpu.VMEM((tables * slots, emb, rows), jnp.bfloat16),
            pltpu.VMEM((1, units), jnp.bfloat16),
            pltpu.VMEM((1, units), jnp.bfloat16),
            pltpu.SemaphoreType.DMA((4,)),
        ],
        compiler_params=pltpu.CompilerParams(vmem_limit_bytes=VMEM_LIMIT),
        cost_estimate=pl.CostEstimate(
            flops=4 * rows * depth * units,
            bytes_accessed=2 * depth * units,
            transcendentals=rows * units,
        ),
    )(slot_of, feats, w, in_hbm(b), in_hbm(h))
    grads = list(results[3:])
    return *results[:3], [[grads.pop(0) for _ in sizes] for sizes in pieces]


def teacher_body(pieces, slot_of, *refs):
    count = sum(pieces)
    sources, (w, b, h, logit, feats, blocks, held, total, here) = list(refs[:count]), refs[count:]
    copies = []
    for k, n in enumerate(pieces):
        first = 0
        for _ in range(n):
            source = sources.pop(0)
            last = first + source.shape[0]
            copies.append(
                pltpu.make_async_copy(source, blocks.at[k, first:last], here.at[len(copies)])
            )
            first = last
    for copy in copies:
        copy.start()
    for copy in copies:
        copy.wait()
    copy_features(slot_of, blocks, feats)
    total[...] = jnp.zeros_like(total)

    def finish(i, pre):
        head = h[:, part_of(i, pre.shape[1])].astype(jnp.float32)
        add_lanes(total, swish(pre)[1] * head)

    forward_tiles(feats, w, b, held, finish)
    logit[...] = jnp.sum(total[...].T, axis=0, keepdims=True)


def teacher(slot_of, blocks, w, b, h):
    _, rows, emb = blocks[0][0].shape
    slots = sum(piece.shape[0] for piece in blocks[0])
    depth, units = w.shape
    pieces = [len(block) for block in blocks]
    count = sum(pieces)
    return pl.pallas_call(
        functools.partial(teacher_body, pieces),
        in_specs=[SMEM] + [pl.BlockSpec(memory_space=pl.ANY)] * count + [VMEM] * 3,
        out_specs=VMEM,
        out_shape=jax.ShapeDtypeStruct((1, rows), jnp.float32),
        scratch_shapes=[
            pltpu.VMEM((rows, depth), jnp.bfloat16),
            pltpu.VMEM((len(blocks), slots, rows, emb), jnp.bfloat16),
            pltpu.VMEM((rows, tiles(units)), jnp.float32),
            pltpu.VMEM((rows, 128), jnp.float32),
            pltpu.SemaphoreType.DMA((count,)),
        ],
        compiler_params=pltpu.CompilerParams(vmem_limit_bytes=VMEM_LIMIT),
        cost_estimate=pl.CostEstimate(
            flops=2 * rows * depth * units,
            bytes_accessed=2 * depth * units,
            transcendentals=rows * units,
        ),
    )(slot_of, *(piece for block in blocks for piece in block), w, b, h)


def rows_body(count, y_ref, *refs):
    zs, ts, refs = refs[:count], refs[count : 2 * count], refs[2 * count :]
    slope, active_in, low, bias, head, loss, scale, active, here = refs
    rows = y_ref.shape[1]
    fetch = pltpu.make_async_copy(active_in, active, here)
    fetch.start()
    z = zs[0][...]
    if count == 2:
        z = z + from_terms(zs[1][zs[1].shape[0] - 1, :16, :])
    soft = jax.nn.sigmoid(sum(ref[...] for ref in ts))
    y = y_ref[...].astype(jnp.float32)
    grads = 2.0 * jax.nn.sigmoid(z) - y - soft
    scale[...] = grads
    softplus = jnp.maximum(z, 0.0) + jnp.log1p(jnp.exp(-jnp.abs(z)))
    losses = 2.0 * softplus - y * z - soft * z
    loss[...] = jnp.sum(losses, axis=1, keepdims=True) / rows
    column = jnp.broadcast_to(grads, (128, rows)).T

    @pl.loop(0, slope.shape[1] // 512)
    def _(i):
        for j in range(4):
            cut = part_of(4 * i + j, 128)
            pre = slope[:, cut].astype(jnp.float32) * column
            low[:, cut] = pre.astype(jnp.bfloat16)
            bias[:, cut] = jnp.sum(pre, axis=0, keepdims=True)

    fetch.wait()

    @pl.loop(0, slope.shape[1] // 512)
    def _(i):
        for j in range(4):
            cut = part_of(4 * i + j, 128)
            head[:, cut] = jnp.sum(
                active[:, cut].astype(jnp.float32) * column, axis=0, keepdims=True
            )


def row_grads(z_parts, t_parts, labels, slope, active):
    rows, units = slope.shape
    shape = jax.ShapeDtypeStruct
    row, units_row = whole((1, rows)), whole((1, units))
    return pl.pallas_call(
        functools.partial(rows_body, len(z_parts)),
        grid=(1,),
        in_specs=[row] * 2 + [VMEM] * (len(z_parts) - 1) + [row] * len(t_parts) + [VMEM, HBM],
        out_specs=[VMEM, units_row, units_row, whole((1, 1)), row],
        out_shape=[
            shape((rows, units), jnp.bfloat16),
            shape((1, units), jnp.float32),
            shape((1, units), jnp.float32),
            shape((1, 1), jnp.float32),
            shape((1, rows), jnp.float32),
        ],
        scratch_shapes=[pltpu.VMEM((rows, units), jnp.bfloat16), pltpu.SemaphoreType.DMA],
        compiler_params=pltpu.CompilerParams(vmem_limit_bytes=VMEM_LIMIT),
    )(in_hbm(labels), *z_parts, *t_parts, slope, in_hbm(active))


def scaled_body(sizes, scale, kept, *refs):
    others, out = refs[:-1], refs[-1]
    factor, first = scale[...], 0
    for i, size in enumerate(sizes):
        cut = slice(first, first + size)
        total = kept[cut].astype(jnp.float32)
        for piece in others[i :: len(sizes)]:
            total = total + piece[:size].astype(jnp.float32)
        out[cut] = (total * factor).astype(jnp.bfloat16)
        first += size


def scaled_sum(scale, kept, others):
    slots, emb, rows = kept.shape
    last = [piece.shape[0] for piece in others[0][1:]]
    sizes = [slots - sum(last)] + last
    flat = [piece for pieces in others for piece in pieces]
    return pl.pallas_call(
        functools.partial(scaled_body, sizes),
        in_specs=[VMEM] * (2 + len(flat)),
        out_specs=VMEM,
        out_shape=jax.ShapeDtypeStruct((slots, emb, rows), jnp.bfloat16),
        compiler_params=pltpu.CompilerParams(vmem_limit_bytes=VMEM_LIMIT),
    )(scale.reshape(1, 1, rows), kept, *flat)


def across(value, shift):
    count = lax.axis_size("table")
    return lax.ppermute(value, "table", [(i, (i + shift) % count) for i in range(count)])


def swap(bits, value, shift=0):
    copies, tables = lax.axis_size("copy"), lax.axis_size("table")
    pairs = [
        (c * tables + i, (c ^ bits) * tables + (i + shift) % tables)
        for c in range(copies)
        for i in range(tables)
    ]
    return lax.ppermute(value, ("copy", "table"), pairs)


def after(value, other):
    return lax.optimization_barrier((value, other))[0]


def by_distance(run, distance, *values):
    branches = [functools.partial(run, bits) for bits in range(1, lax.axis_size("copy"))]
    return lax.switch(distance - 1, branches, *values)


def swap_rows(bits, own, slot_of, w):
    cut = (2 * own.shape[0]) // 7
    first = swap(bits, own[:cut])
    second = swap(bits, after(own[cut:], first))
    feats = features(slot_of, [own, across(own, 1)])
    return feats, in_vmem(after(w, first)), first, second, across(first, 1)


def swap_logits(bits, t_own):
    return swap(bits, t_own), swap(bits, t_own, 1)


def on_device(pooled, slot_of_table, partner, labels, w_first, b_first, w_head):
    tables = lax.axis_size("table")
    rows, slots, emb = pooled.shape
    me_copy = lax.axis_index("copy")
    distance = jnp.bitwise_xor(me_copy, partner[me_copy])

    own = jnp.transpose(pooled, (1, 0, 2))
    if tables == 2:
        (feats, again), w, first, second, first_other = by_distance(
            swap_rows, distance, own, slot_of_table, w_first[0]
        )
        their_blocks = [[first, second], [first_other, across(second, 1)]]
    else:
        feats, again = features(slot_of_table, [own] + [across(own, k) for k in range(1, tables)])
        w = in_vmem(w_first[0])
        theirs = by_distance(swap, distance, own)
        their_blocks = [[theirs]] + [[across(theirs, k)] for k in range(1, tables)]

    z_own, slope, active, grads = student(slot_of_table, feats, w, b_first, w_head, slots)
    early = [across(pieces[0], k) for k, pieces in enumerate(grads) if k]
    t_own = teacher(slot_of_table, their_blocks, w, b_first, w_head)
    for piece in early:
        t_own = after(t_own, piece)
    if tables == 2:
        t_parts = by_distance(swap_logits, distance, t_own)
        z_parts = [z_own, early[0]]
    else:
        z_own, t_own = lax.psum((z_own, t_own), "table")
        z_parts, t_parts = [z_own], [by_distance(swap, distance, t_own)]
    others = [
        [piece] + [across(after(rest, t_parts[-1]), k) for rest in grads[k][1:]]
        for k, piece in enumerate(early, 1)
    ]

    low, grad_bias, grad_head, loss, scale = row_grads(
        z_parts, t_parts, labels.reshape(1, rows), slope, active
    )
    grad_first = lax.dot_general(
        again, low, (((0,), (0,)), ((), ())), preferred_element_type=jnp.float32
    ).astype(jnp.bfloat16)
    pooled_grad = scaled_sum(scale, grads[0][0], others)
    return (pooled_grad, grad_first[None], grad_bias, grad_head, loss.reshape(1))


def solution(mesh):
    in_specs = (
        P("copy", "table", None),
        P(),
        P(),
        P("copy"),
        P("copy", None, "table"),
        P("copy", "table"),
        P("copy", "table"),
    )
    out_specs = (
        P("table", None, "copy"),
        P("copy", None, "table"),
        P("copy", "table"),
        P("copy", "table"),
        P("copy"),
    )
    return jax.shard_map(
        on_device, mesh=mesh, in_specs=in_specs, out_specs=out_specs, check_vma=False
    )
```

```python
import functools

import jax
import jax.numpy as jnp
from jax import lax
from jax.experimental import pallas as pl
from jax.experimental.pallas import tpu as pltpu
from jax.sharding import PartitionSpec as P

VMEM_LIMIT = 12 * 1024 * 1024
VMEM = pl.BlockSpec(memory_space=pltpu.VMEM)
SMEM = pl.BlockSpec(memory_space=pltpu.SMEM)
HBM = pl.BlockSpec(memory_space=pltpu.HBM)
TILE = 256


def in_hbm(value):
    return pltpu.with_memory_space_constraint(value, pltpu.HBM)


def whole(shape):
    return pl.BlockSpec(shape, lambda *_: (0,) * len(shape))


def tiles(width):
    return TILE if width % TILE == 0 else width


def part_of(i, size):
    return pl.ds(pl.multiple_of(i * size, size), size)


def copy_features(slot_of, blocks, feats):
    me = lax.axis_index("table")
    tables, slots, _, emb = blocks.shape

    @pl.loop(0, feats.shape[1] // emb)
    def _(t):
        slot = slot_of[t]
        group = lax.rem(me + tables - slot // slots, tables)
        feats[:, part_of(t, emb)] = blocks[group, lax.rem(slot, slots)]


def forward_tiles(feats, w, b, held, finish):
    tile = held.shape[1]
    count = w.shape[1] // tile

    def product(i):
        cut = part_of(i, tile)
        value = jnp.dot(feats[...], w[:, cut], preferred_element_type=jnp.float32)
        return value + b[:, cut].astype(jnp.float32)

    held[...] = product(0)

    @pl.loop(1, count)
    def _(i):
        before = held[...]
        value = product(i)
        finish(i - 1, before)
        held[...] = value

    finish(count - 1, held[...])


def swish(pre):
    sigmoid = 0.5 * jnp.tanh(0.5 * pre) + 0.5
    return sigmoid, pre * sigmoid


def add_lanes(total, wide):
    for lane in range(0, wide.shape[1], 128):
        total[...] += wide[:, lane : lane + 128]


def in_terms(row):
    high = row.astype(jnp.bfloat16).astype(jnp.float32)
    middle = (row - high).astype(jnp.bfloat16).astype(jnp.float32)
    at = lax.broadcasted_iota(jnp.int32, (16, row.shape[1]), 0)
    terms = jnp.where(at == 0, high, jnp.where(at == 1, middle, row - high - middle))
    return terms.astype(jnp.bfloat16)


def from_terms(terms):
    wide = terms.astype(jnp.float32)
    return wide[0:1] + wide[1:2] + wide[2:3]


def load_body(source, goal, here):
    copy = pltpu.make_async_copy(source, goal, here)
    copy.start()
    copy.wait()


def in_vmem(value):
    return pl.pallas_call(
        load_body,
        in_specs=[HBM],
        out_specs=VMEM,
        out_shape=jax.ShapeDtypeStruct(value.shape, value.dtype),
        scratch_shapes=[pltpu.SemaphoreType.DMA],
        compiler_params=pltpu.CompilerParams(vmem_limit_bytes=1024 * 1024),
    )(in_hbm(value))


def features_body(slot_of, *refs):
    sources, (feats, again, blocks, here) = refs[:-4], refs[-4:]
    copies = [
        pltpu.make_async_copy(source, blocks.at[k], here.at[k])
        for k, source in enumerate(sources)
    ]
    for copy in copies:
        copy.start()
    for copy in copies:
        copy.wait()
    copy_features(slot_of, blocks, feats)
    again[...] = feats[...]


def features(slot_of, blocks):
    slots, rows, emb = blocks[0].shape
    depth = slot_of.shape[0] * emb
    return pl.pallas_call(
        features_body,
        in_specs=[SMEM] + [pl.BlockSpec(memory_space=pl.ANY)] * len(blocks),
        out_specs=[VMEM] * 2,
        out_shape=[jax.ShapeDtypeStruct((rows, depth), jnp.bfloat16)] * 2,
        scratch_shapes=[
            pltpu.VMEM((len(blocks), slots, rows, emb), jnp.bfloat16),
            pltpu.SemaphoreType.DMA((len(blocks),)),
        ],
        compiler_params=pltpu.CompilerParams(vmem_limit_bytes=6 * 1024 * 1024),
    )(slot_of, *blocks)


def student_body(pieces, slot_of, *refs):
    feats, w, b_in, h_in, logit, slope, active_out, *refs = refs
    grads = [[refs.pop(0) for _ in sizes] for sizes in pieces]
    carried = grads[1][0] if len(pieces) == 2 else None
    held, total, turned, active, every, b, h, here = refs
    slots, emb, _ = grads[0][0].shape
    small = [
        pltpu.make_async_copy(b_in, b, here.at[0]),
        pltpu.make_async_copy(h_in, h, here.at[1]),
    ]
    for copy in small:
        copy.start()
    for copy in small:
        copy.wait()
    total[...] = jnp.zeros_like(total)

    def finish(i, pre):
        cut = part_of(i, pre.shape[1])
        head = h[:, cut].astype(jnp.float32)
        sigmoid, act = swish(pre)
        add_lanes(total, act * head)
        low = (head * (sigmoid + act * (1.0 - sigmoid))).astype(jnp.bfloat16)
        slope[:, cut] = low
        turned[cut, :] = low.T
        active[:, cut] = act.astype(jnp.bfloat16)

    forward_tiles(feats, w, b, held, finish)
    logit[...] = jnp.sum(total[...].T, axis=0, keepdims=True)

    keep = pltpu.make_async_copy(active, active_out, here.at[len(small)])
    keep.start()
    every[...] = jnp.zeros_like(every)
    if carried is not None:
        carried[carried.shape[0] - 16 :, :] = in_terms(logit[...])

    me, tables = lax.axis_index("table"), lax.axis_size("table")
    used = w.shape[0] // emb
    group = max(n for n in range(1, 14) if used % n == 0)

    @pl.loop(0, used // group)
    def _(i):
        value = jnp.dot(
            w[part_of(i, group * emb), :], turned[...], preferred_element_type=jnp.float32
        ).astype(jnp.bfloat16)
        for j in range(group):
            slot = slot_of[group * i + j]
            owner = lax.rem(slot // slots + tables - me, tables)
            every[owner * slots + lax.rem(slot, slots)] = value[j * emb : (j + 1) * emb, :]

    kept = pltpu.make_async_copy(every.at[:slots], grads[0][0], here.at[len(small) + 1])
    kept.start()
    for k in range(1, len(pieces)):
        first = k * slots
        for grad, size in zip(grads[k], pieces[k]):
            value = every[first : first + size]
            grad[: size * emb, :] = value.reshape(size * emb, value.shape[2])
            first += size

    kept.wait()
    keep.wait()


def student(slot_of, feats, w, b, h, slots):
    rows, depth = feats.shape
    units = w.shape[1]
    emb = depth // slot_of.shape[0]
    tables = lax.axis_size("table")
    first = (3 * slots) // 7
    sizes = [first, slots - first] if tables == 2 else [slots]
    pieces = [[slots]] + [sizes] * (tables - 1)
    shape = jax.ShapeDtypeStruct
    results = pl.pallas_call(
        functools.partial(student_body, pieces),
        in_specs=[SMEM, VMEM, VMEM, HBM, HBM],
        out_specs=[VMEM, VMEM, HBM, HBM] + [VMEM] * sum(len(sizes) for sizes in pieces[1:]),
        out_shape=[
            shape((1, rows), jnp.float32),
            shape((rows, units), jnp.bfloat16),
            pltpu.HBM((rows, units), jnp.bfloat16),
            pltpu.HBM((slots, emb, rows), jnp.bfloat16),
        ]
        + [
            shape((size * emb + 16 * (tables == 2 and j == 0), rows), jnp.bfloat16)
            for sizes in pieces[1:]
            for j, size in enumerate(sizes)
        ],
        scratch_shapes=[
            pltpu.VMEM((rows, tiles(units)), jnp.float32),
            pltpu.VMEM((rows, 128), jnp.float32),
            pltpu.VMEM((units, rows), jnp.bfloat16),
            pltpu.VMEM((rows, units), jnp.bfloat16),
            pltpu.VMEM((tables * slots, emb, rows), jnp.bfloat16),
            pltpu.VMEM((1, units), jnp.bfloat16),
            pltpu.VMEM((1, units), jnp.bfloat16),
            pltpu.SemaphoreType.DMA((4,)),
        ],
        compiler_params=pltpu.CompilerParams(vmem_limit_bytes=VMEM_LIMIT),
        cost_estimate=pl.CostEstimate(
            flops=4 * rows * depth * units,
            bytes_accessed=2 * depth * units,
            transcendentals=rows * units,
        ),
    )(slot_of, feats, w, in_hbm(b), in_hbm(h))
    grads = list(results[3:])
    return *results[:3], [[grads.pop(0) for _ in sizes] for sizes in pieces]


def teacher_body(pieces, slot_of, *refs):
    count = sum(pieces)
    sources, (w, b, h, logit, feats, blocks, held, total, here) = list(refs[:count]), refs[count:]
    copies = []
    for k, n in enumerate(pieces):
        first = 0
        for _ in range(n):
            source = sources.pop(0)
            last = first + source.shape[0]
            copies.append(
                pltpu.make_async_copy(source, blocks.at[k, first:last], here.at[len(copies)])
            )
            first = last
    for copy in copies:
        copy.start()
    for copy in copies:
        copy.wait()
    copy_features(slot_of, blocks, feats)
    total[...] = jnp.zeros_like(total)

    def finish(i, pre):
        head = h[:, part_of(i, pre.shape[1])].astype(jnp.float32)
        add_lanes(total, swish(pre)[1] * head)

    forward_tiles(feats, w, b, held, finish)
    logit[...] = jnp.sum(total[...].T, axis=0, keepdims=True)


def teacher(slot_of, blocks, w, b, h):
    _, rows, emb = blocks[0][0].shape
    slots = sum(piece.shape[0] for piece in blocks[0])
    depth, units = w.shape
    pieces = [len(block) for block in blocks]
    count = sum(pieces)
    return pl.pallas_call(
        functools.partial(teacher_body, pieces),
        in_specs=[SMEM] + [pl.BlockSpec(memory_space=pl.ANY)] * count + [VMEM] * 3,
        out_specs=VMEM,
        out_shape=jax.ShapeDtypeStruct((1, rows), jnp.float32),
        scratch_shapes=[
            pltpu.VMEM((rows, depth), jnp.bfloat16),
            pltpu.VMEM((len(blocks), slots, rows, emb), jnp.bfloat16),
            pltpu.VMEM((rows, tiles(units)), jnp.float32),
            pltpu.VMEM((rows, 128), jnp.float32),
            pltpu.SemaphoreType.DMA((count,)),
        ],
        compiler_params=pltpu.CompilerParams(vmem_limit_bytes=VMEM_LIMIT),
        cost_estimate=pl.CostEstimate(
            flops=2 * rows * depth * units,
            bytes_accessed=2 * depth * units,
            transcendentals=rows * units,
        ),
    )(slot_of, *(piece for block in blocks for piece in block), w, b, h)


def rows_body(count, y_ref, *refs):
    zs, ts, refs = refs[:count], refs[count : 2 * count], refs[2 * count :]
    slope, active_in, low, bias, head, loss, scale, active, here = refs
    rows = y_ref.shape[1]
    fetch = pltpu.make_async_copy(active_in, active, here)
    fetch.start()
    z = zs[0][...]
    if count == 2:
        z = z + from_terms(zs[1][zs[1].shape[0] - 16 :, :])
    soft = jax.nn.sigmoid(sum(ref[...] for ref in ts))
    y = y_ref[...].astype(jnp.float32)
    grads = 2.0 * jax.nn.sigmoid(z) - y - soft
    scale[...] = grads
    softplus = jnp.maximum(z, 0.0) + jnp.log1p(jnp.exp(-jnp.abs(z)))
    losses = 2.0 * softplus - y * z - soft * z
    loss[...] = jnp.sum(losses, axis=1, keepdims=True) / rows
    column = jnp.broadcast_to(grads, (128, rows)).T

    @pl.loop(0, slope.shape[1] // 512)
    def _(i):
        for j in range(4):
            cut = part_of(4 * i + j, 128)
            pre = slope[:, cut].astype(jnp.float32) * column
            low[:, cut] = pre.astype(jnp.bfloat16)
            bias[:, cut] = jnp.sum(pre, axis=0, keepdims=True)

    fetch.wait()

    @pl.loop(0, slope.shape[1] // 512)
    def _(i):
        for j in range(4):
            cut = part_of(4 * i + j, 128)
            head[:, cut] = jnp.sum(
                active[:, cut].astype(jnp.float32) * column, axis=0, keepdims=True
            )


def row_grads(z_parts, t_parts, labels, slope, active):
    rows, units = slope.shape
    shape = jax.ShapeDtypeStruct
    row, units_row = whole((1, rows)), whole((1, units))
    return pl.pallas_call(
        functools.partial(rows_body, len(z_parts)),
        grid=(1,),
        in_specs=[row] * 2 + [VMEM] * (len(z_parts) - 1) + [row] * len(t_parts) + [VMEM, HBM],
        out_specs=[VMEM, units_row, units_row, whole((1, 1)), row],
        out_shape=[
            shape((rows, units), jnp.bfloat16),
            shape((1, units), jnp.float32),
            shape((1, units), jnp.float32),
            shape((1, 1), jnp.float32),
            shape((1, rows), jnp.float32),
        ],
        scratch_shapes=[pltpu.VMEM((rows, units), jnp.bfloat16), pltpu.SemaphoreType.DMA],
        compiler_params=pltpu.CompilerParams(vmem_limit_bytes=VMEM_LIMIT),
    )(in_hbm(labels), *z_parts, *t_parts, slope, in_hbm(active))


def scaled_body(sizes, scale, kept, *refs):
    others, out = refs[:-1], refs[-1]
    factor, first = scale[...], 0
    for i, size in enumerate(sizes):
        cut = slice(first, first + size)
        total = kept[cut].astype(jnp.float32)
        for piece in others[i :: len(sizes)]:
            value = piece[: size * kept.shape[1], :].astype(jnp.float32)
            total = total + value.reshape(total.shape)
        out[cut] = (total * factor).astype(jnp.bfloat16)
        first += size


def scaled_sum(scale, kept, others):
    slots, emb, rows = kept.shape
    last = [piece.shape[0] // emb for piece in others[0][1:]]
    sizes = [slots - sum(last)] + last
    flat = [piece for pieces in others for piece in pieces]
    return pl.pallas_call(
        functools.partial(scaled_body, sizes),
        in_specs=[VMEM] * (2 + len(flat)),
        out_specs=VMEM,
        out_shape=jax.ShapeDtypeStruct((slots, emb, rows), jnp.bfloat16),
        compiler_params=pltpu.CompilerParams(vmem_limit_bytes=VMEM_LIMIT),
    )(scale.reshape(1, 1, rows), kept, *flat)


def across(value, shift):
    count = lax.axis_size("table")
    return lax.ppermute(value, "table", [(i, (i + shift) % count) for i in range(count)])


def swap(bits, value, shift=0):
    copies, tables = lax.axis_size("copy"), lax.axis_size("table")
    pairs = [
        (c * tables + i, (c ^ bits) * tables + (i + shift) % tables)
        for c in range(copies)
        for i in range(tables)
    ]
    return lax.ppermute(value, ("copy", "table"), pairs)


def after(value, other):
    return lax.optimization_barrier((value, other))[0]


def by_distance(run, distance, *values):
    branches = [functools.partial(run, bits) for bits in range(1, lax.axis_size("copy"))]
    return lax.switch(distance - 1, branches, *values)


def swap_rows(bits, own, slot_of, w):
    cut = own.shape[0] // 2
    first = swap(bits, own[:cut])
    second = swap(bits, after(own[cut:], first))
    feats = features(slot_of, [own, across(own, 1)])
    return feats, in_vmem(after(w, first)), first, second, across(first, 1)


def swap_logits(bits, t_own):
    return swap(bits, t_own), swap(bits, t_own, 1)


def on_device(pooled, slot_of_table, partner, labels, w_first, b_first, w_head):
    tables = lax.axis_size("table")
    rows, slots, emb = pooled.shape
    me_copy = lax.axis_index("copy")
    distance = jnp.bitwise_xor(me_copy, partner[me_copy])

    own = jnp.transpose(pooled, (1, 0, 2))
    if tables == 2:
        (feats, again), w, first, second, first_other = by_distance(
            swap_rows, distance, own, slot_of_table, w_first[0]
        )
        their_blocks = [[first, second], [first_other, across(second, 1)]]
    else:
        feats, again = features(slot_of_table, [own] + [across(own, k) for k in range(1, tables)])
        w = in_vmem(w_first[0])
        theirs = by_distance(swap, distance, own)
        their_blocks = [[theirs]] + [[across(theirs, k)] for k in range(1, tables)]

    z_own, slope, active, grads = student(slot_of_table, feats, w, b_first, w_head, slots)
    early = [across(pieces[0], k) for k, pieces in enumerate(grads) if k]
    t_own = teacher(slot_of_table, their_blocks, w, b_first, w_head)
    for piece in early:
        t_own = after(t_own, piece)
    if tables == 2:
        t_parts = by_distance(swap_logits, distance, t_own)
        z_parts = [z_own, early[0]]
    else:
        z_own, t_own = lax.psum((z_own, t_own), "table")
        z_parts, t_parts = [z_own], [by_distance(swap, distance, t_own)]
    others = [
        [piece] + [across(after(rest, t_parts[-1]), k) for rest in grads[k][1:]]
        for k, piece in enumerate(early, 1)
    ]

    low, grad_bias, grad_head, loss, scale = row_grads(
        z_parts, t_parts, labels.reshape(1, rows), slope, active
    )
    grad_first = lax.dot_general(
        again, low, (((0,), (0,)), ((), ())), preferred_element_type=jnp.float32
    ).astype(jnp.bfloat16)
    pooled_grad = scaled_sum(scale, grads[0][0], others)
    return (pooled_grad, grad_first[None], grad_bias, grad_head, loss.reshape(1))


def solution(mesh):
    in_specs = (
        P("copy", "table", None),
        P(),
        P(),
        P("copy"),
        P("copy", None, "table"),
        P("copy", "table"),
        P("copy", "table"),
    )
    out_specs = (
        P("table", None, "copy"),
        P("copy", None, "table"),
        P("copy", "table"),
        P("copy", "table"),
        P("copy"),
    )
    return jax.shard_map(
        on_device, mesh=mesh, in_specs=in_specs, out_specs=out_specs, check_vma=False
    )
```
